512 devices in a mesh: view: 32 (over y, z_lo), eye: 2 (over z_hi), seq: 8 (over x, core).
Axes of the slice: x: 4, y: 4, z: 16 (z_hi: 2, z_lo: 8; z = z_hi * 8 + z_lo), core: 2. Of those that a mesh axis runs over, the one named last changes fastest.
Arguments:
- queries: bfloat16 [32, 2, 1024, 4096], P('view', 'eye', 'seq'), may hold values from -6 to 6
- keys: bfloat16 [32, 2, 1024, 4096], P('view', 'eye', 'seq'), may hold values from -6 to 6
- values: bfloat16 [32, 2, 1024, 4096], P('view', 'eye', 'seq'), may hold values from -60 to 60
- fwd_index: int32 [32, 2, 4, 3072], P('view', 'eye'), may hold values from 0 to 127
- fwd_weight: float32 [32, 2, 4, 3072], P('view', 'eye'), may hold values from 0.1 to 1
- own_map: int32 [32, 2, 2, 1024], P('view', 'eye'), may hold values 0 or 1
- back_index: int32 [32, 2, 4, 1024], P('view', 'eye'), may hold values from 0 to 383
- back_weight: float32 [32, 2, 4, 1024], P('view', 'eye'), may hold values from 0.1 to 1
- head_gain: float32 [4096], replicated, may hold values from 0.1 to 1.9
- head_shift: float32 [4096], replicated, may hold values from -3 to 3
- head_weight: bfloat16 [4096, 64], replicated, may hold values from -0.09375 to 0.09375
- latents: float32 [32, 2, 64, 1024], P('view', 'eye', None, 'seq'), may hold values from -6 to 6
- eye_mix: float32 [64], replicated, may hold values from 0.2 to 0.5
Outputs:
- updated: float32 [32, 2, 64, 1024], P('view', 'eye', None, 'seq')
The draws below stay inside these ranges and needn't reach their ends.
All inputs are finite; a program needn't handle non-finite values. No bound on the sum of `own_map` on one device may be relied on, other than what follows from the above.
Results may differ from the reference program's by a relative error of at most 0.007.
Values may be sent and summed in bfloat16 or wider, within the bound.
A program may use at most 64 MiB of HBM per device.

```python
import math
import jax
import jax.numpy as jnp
from jax import lax

HEADS = 32
DH = 128
LAT = 64
TOK_DEV = 128
SEQ_VIEW = 1024
N_VIEW = 32
N_EYE = 2
N_SEQ = 8


def draw_queries(key, part):
    key = jax.random.fold_in(key, 11)
    shape = (N_VIEW, N_EYE, SEQ_VIEW, HEADS, DH)
    result = jnp.clip(jax.random.normal(key, shape, jnp.float32), -6.0, 6.0)
    return result.reshape(N_VIEW, N_EYE, SEQ_VIEW, HEADS * DH).astype(jnp.bfloat16)


def draw_keys(key, part):
    key = jax.random.fold_in(key, 12)
    shape = (N_VIEW, N_EYE, SEQ_VIEW, HEADS, DH)
    result = jnp.clip(jax.random.normal(key, shape, jnp.float32), -6.0, 6.0)
    return result.reshape(N_VIEW, N_EYE, SEQ_VIEW, HEADS * DH).astype(jnp.bfloat16)


def draw_values(key, part):
    key = jax.random.fold_in(key, 13)
    first = jax.random.fold_in(key, 0)
    shape = (N_VIEW, N_EYE, SEQ_VIEW, HEADS * DH)
    result = jnp.clip(jax.random.normal(first, shape, jnp.float32), -6.0, 6.0)
    return result.astype(jnp.bfloat16)


def touch_ends(values, own_key, low, largest):
    longest = values.shape.index(max(values.shape))
    spots = []
    for shift in (0, 1):
        where = [jax.random.randint(jax.random.fold_in(own_key, axis), (), 0, length) for axis, length in enumerate(values.shape)]
        where[longest] = (where[longest] + shift) % values.shape[longest]
        spots.append(tuple(where))
    return values.at[spots[0]].set(low).at[spots[1]].set(largest)


def block_scale(own_key, extent, shards, least, largest):
    def one(position, blocks):
        steps = jax.random.uniform(jax.random.fold_in(jax.random.fold_in(own_key, 6), position), (blocks,), jnp.float32, least / len(shards), largest / len(shards))
        return jnp.repeat(jnp.exp(steps), extent[position] // blocks).reshape((-1,) + (1,) * (len(extent) - position - 1))

    gain = one(*shards[0])
    for cut in shards[1:]:
        gain = gain * one(*cut)
    return gain


def gaussian(rng, extent, scale, reach, cuts=(), kind=jnp.bfloat16):
    drawn = jax.random.normal(rng, extent, jnp.float32) * scale
    if len(cuts) > 0:
        drawn = block_scale(rng, extent, cuts, -0.22, 0.18) * drawn
    return jnp.clip(drawn, min=-reach, max=reach).astype(kind)


def setup_inputs(seed: int = 0) -> dict:
    streams_of = jax.random.split(jax.random.key(seed), 14)
    return {
        "queries": draw_queries(jax.random.fold_in(streams_of[13], 71), 0),
        "keys": draw_keys(jax.random.fold_in(streams_of[13], 71), 0),
        "values": draw_values(jax.random.fold_in(streams_of[13], 71), 0),
        "fwd_index": touch_ends(jax.random.randint(streams_of[3], (N_VIEW, N_EYE, 4, 3 * SEQ_VIEW), 0, TOK_DEV), jax.random.fold_in(streams_of[3], 1), 0, TOK_DEV - 1).astype(jnp.int32),
        "fwd_weight": jnp.clip(0.1 + 0.9 * jax.random.uniform(streams_of[4], (N_VIEW, N_EYE, 4, 3 * SEQ_VIEW), jnp.float32) ** block_scale(streams_of[4], (N_VIEW, N_EYE, 4, 3 * SEQ_VIEW), ((0, 32), (1, 2)), -0.2, 0.2), 0.1, 1.0),
        "own_map": touch_ends((jax.random.randint(streams_of[5], (N_VIEW, N_EYE, 2, SEQ_VIEW), 0, 3) < 2).astype(jnp.int32), jax.random.fold_in(streams_of[5], 1), 0, 1),
        "back_index": touch_ends(jax.random.randint(streams_of[6], (N_VIEW, N_EYE, 4, SEQ_VIEW), 0, 3 * TOK_DEV), jax.random.fold_in(streams_of[6], 1), 0, (3 * TOK_DEV) - 1).astype(jnp.int32),
        "back_weight": jnp.clip(0.1 + 0.9 * jax.random.uniform(streams_of[7], (N_VIEW, N_EYE, 4, SEQ_VIEW), jnp.float32) ** block_scale(streams_of[7], (N_VIEW, N_EYE, 4, SEQ_VIEW), ((0, 32), (1, 2)), -0.2, 0.2), 0.1, 1.0),
        "head_gain": jnp.clip(1.0 + 0.18 * jax.random.normal(streams_of[8], (HEADS * DH,), jnp.float32), 0.1, 1.9),
        "head_shift": gaussian(streams_of[9], (HEADS * DH,), 0.5, 3.0, (), jnp.float32),
        "head_weight": gaussian(streams_of[10], (HEADS * DH, LAT), (HEADS * DH) ** -0.5, 0.09375),
        "latents": gaussian(streams_of[11], (N_VIEW, N_EYE, LAT, SEQ_VIEW), 1.0, 6.0, ((0, 32), (1, 2), (3, 8)), jnp.float32),
        "eye_mix": jnp.clip(jax.random.uniform(streams_of[12], (LAT,), jnp.float32, 0.2, 0.5), 0.2, 0.5),
    }


def pick(block, index):
    return jax.vmap(lambda part, rows: jnp.take(part, rows, axis=0))(block, index)

def attend_sequence(query, keyset, valueset):
    length = query.shape[0]
    block = min(512, length)
    scale = 1.0 / math.sqrt(DH)
    keys_wide = keyset.reshape(length, HEADS, DH).astype(jnp.float32)
    values_wide = valueset.reshape(length, HEADS, DH).astype(jnp.float32)

    def one_block(rows):
        scores = jnp.einsum('qhd,khd->hqk', rows.astype(jnp.float32), keys_wide) * scale
        highest = lax.optimization_barrier(jnp.max(scores, axis=2, keepdims=True))
        probs = jnp.exp(scores - highest)
        total = lax.optimization_barrier(jnp.sum(probs, axis=2))
        rounded = lax.optimization_barrier(probs.astype(jnp.bfloat16))
        mixed = jnp.einsum('hqk,khd->qhd', rounded.astype(jnp.float32), values_wide)
        return (mixed / jnp.transpose(total)[:, :, None]).astype(jnp.bfloat16)
    blocks_all = query.reshape(length // block, block, HEADS, DH)
    return lax.map(one_block, blocks_all).reshape(length, HEADS * DH)

def reference(queries, keys, values, fwd_index, fwd_weight, own_map, back_index, back_weight, head_gain, head_shift, head_weight, latents, eye_mix):
    width = HEADS * DH
    flat = (queries.reshape(N_VIEW * N_EYE, SEQ_VIEW, width), keys.reshape(N_VIEW * N_EYE, SEQ_VIEW, width), values.reshape(N_VIEW * N_EYE, SEQ_VIEW, width))
    attended = lax.map(lambda parts: attend_sequence(parts[0], parts[1], parts[2]), flat)
    attended = attended.reshape(N_VIEW, N_EYE, N_SEQ, TOK_DEV, width)
    views = jnp.arange(N_VIEW, dtype=jnp.int32)
    weight_full = head_weight.astype(jnp.float32)

    def contribute(view_now):
        source = attended[view_now]
        index_now = fwd_index[view_now].reshape(N_EYE, 4, N_SEQ, 3 * TOK_DEV)
        weight_now = fwd_weight[view_now].reshape(N_EYE, 4, N_SEQ, 3 * TOK_DEV)
        weight_now = weight_now / lax.optimization_barrier(jnp.sum(weight_now, axis=1, keepdims=True))
        summed = jnp.zeros((N_EYE, N_SEQ, 3 * TOK_DEV, width), jnp.float32)
        for tap in range(4):
            taken = jax.vmap(pick)(source, index_now[:, tap]).astype(jnp.float32)
            summed = summed + weight_now[:, tap, :, :, None] * taken
        return summed.astype(jnp.bfloat16)
    contrib = lax.map(contribute, views)

    def join_tile(view_now):
        before = (view_now - 1) % N_VIEW
        after = (view_now + 1) % N_VIEW
        centre = contrib[view_now][:, :, TOK_DEV:2 * TOK_DEV].astype(jnp.float32)
        from_prev = contrib[before][:, :, 2 * TOK_DEV:].astype(jnp.float32)
        from_next = contrib[after][:, :, :TOK_DEV].astype(jnp.float32)
        present = own_map[view_now].reshape(N_EYE, 2, N_SEQ, TOK_DEV).astype(jnp.float32)
        summed = centre + present[:, 0, :, :, None] * from_prev + present[:, 1, :, :, None] * from_next
        return (summed / (1.0 + present[:, 0] + present[:, 1])[..., None]).astype(jnp.bfloat16)
    joined = lax.map(join_tile, views)

    def finish(view_now):
        before = (view_now - 1) % N_VIEW
        after = (view_now + 1) % N_VIEW
        extended = jnp.concatenate([joined[before], joined[view_now], joined[after]], axis=2)
        index_now = back_index[view_now].reshape(N_EYE, 4, N_SEQ, TOK_DEV)
        weight_now = back_weight[view_now].reshape(N_EYE, 4, N_SEQ, TOK_DEV)
        weight_now = weight_now / lax.optimization_barrier(jnp.sum(weight_now, axis=1, keepdims=True))
        summed = jnp.zeros((N_EYE, N_SEQ, TOK_DEV, width), jnp.float32)
        for tap in range(4):
            taken = jax.vmap(pick)(extended, index_now[:, tap]).astype(jnp.float32)
            summed = summed + weight_now[:, tap, :, :, None] * taken
        blended = summed.astype(jnp.bfloat16).reshape(N_EYE, SEQ_VIEW, width).astype(jnp.float32)
        centre_mean = lax.optimization_barrier(jnp.mean(blended, axis=2, keepdims=True))
        centred = blended - centre_mean
        variance = lax.optimization_barrier(jnp.mean(centred * centred, axis=2, keepdims=True))
        normed = centred / jnp.sqrt(variance + 1e-06) * head_gain + head_shift
        velocity = jnp.stack([jnp.transpose(jnp.dot(normed[side], weight_full, precision=lax.Precision.HIGHEST)) for side in range(N_EYE)])
        other = velocity[::-1]
        mixed = velocity + eye_mix[None, :, None] * (other - velocity)
        return latents[view_now] - 0.8 * mixed
    return lax.map(finish, views)
```

```python
import math

import jax
import jax.numpy as jnp
from jax import lax
from jax.experimental import pallas as pl
from jax.experimental.pallas import tpu as pltpu
from jax.sharding import PartitionSpec as P

DH = 128
TOK = 128
SEQ = 8
ROW = 8
HERE = 4
FEAT = HERE * DH
LAT = 64
PACK = 40
MESH = pl.DeviceIdType.MESH
BF = jnp.bfloat16
F32 = jnp.float32


def dot(a, b, dims):
    return lax.dot_general(a, b, (dims, ((), ())), preferred_element_type=F32)


def split(x):
    upper = x.astype(BF)
    return upper, (x - upper.astype(F32)).astype(BF)


def wait(ref, sem):
    pltpu.make_async_copy(ref, ref, sem).wait()


def spread(index, weight, rows):
    places = lax.broadcasted_iota(jnp.int32, (rows, TOK), 0).astype(F32)
    total = jnp.zeros((rows, TOK), F32)
    for tap in range(4):
        total = total + jnp.where(places == index[tap : tap + 1], weight[tap : tap + 1], 0.0)
    return total


def kernel(
    q, k, v, fi_in, fw_in, om_in, bi_in, bw_in, gain_in, shift_in, hw_in, lat_in, mix_in, out,
    fi, fw, om, bi, bw, gain, shift, hw, lat, mix,
    kb, vb, qb, att, ext, pks, pk, vt, jt, mt, acc, stats, wg, gsum, hsum, cols, sp, rp, vs, vsb, vown, voth,
    ins, xs, xr, zs, zr, ys, yr, ps, pr, pys, pyr, rs, rr, fs, fr,
):
    view, eye, seq = lax.axis_index("view"), lax.axis_index("eye"), lax.axis_index("seq")
    row, z = view // ROW, view % ROW
    first = row * ROW
    edge = (z + 2) // 4
    nxt, prv = (view + ROW) % 32, (view + 32 - ROW) % 32
    partner = {"view": first + seq, "eye": eye, "seq": z}
    across = {"view": first + seq, "eye": 1 - eye, "seq": z}

    def along_seq(i):
        return {"view": view, "eye": eye, "seq": i}

    def along_view(i):
        return {"view": i, "eye": eye, "seq": seq}

    def send(src, dst, s, r, target):
        pltpu.make_async_remote_copy(
            src_ref=src, dst_ref=dst, send_sem=s, recv_sem=r, device_id=target, device_id_type=MESH
        ).start()

    def copy(src, dst, s):
        pltpu.make_async_copy(src, dst, s).start()

    small = (
        (fi_in, fi), (fw_in, fw), (om_in, om), (bi_in, bi), (bw_in, bw),
        (gain_in, gain), (shift_in, shift), (hw_in, hw), (lat_in, lat), (mix_in, mix),
    )
    for i, (src, dst) in enumerate(small):
        copy(src, dst, ins.at[i])

    barrier = pltpu.get_barrier_semaphore()

    def greet(target):
        pl.semaphore_signal(barrier, inc=1, device_id=target, device_id_type=MESH)

    for step in range(1, SEQ):
        greet(along_seq((seq + step) % SEQ))
        greet(along_view(first + (z + step) % ROW))
    greet(along_view(nxt))
    greet(along_view(prv))
    greet(across)

    @pl.when(z != seq)
    def _():
        greet(partner)

    pl.semaphore_wait(barrier, 2 * (SEQ - 1) + 3 + jnp.where(z == seq, 0, 1))

    arrays = ((k, kb), (v, vb), (q, qb))

    def send_head(h, core):
        for t, (src, dst) in enumerate(arrays):

            def one(step, _):
                other = (seq // 2 + step) % 4 * 2 + core
                start = pl.multiple_of((other * HERE + h) * DH, DH)
                block = src.at[0, 0, :, pl.ds(start, DH)]

                @pl.when(other != seq)
                def _():
                    send(block, dst.at[h, seq], xs.at[t, h], xr.at[t, h], along_seq(other))

                @pl.when(other == seq)
                def _():
                    copy(block, dst.at[h, seq], xr.at[t, h])

                return 0

            lax.fori_loop(0, 4, one, 0)

    send_head(0, 0)
    send_head(0, 1)

    for i, (src, dst) in enumerate(small):
        pltpu.make_async_copy(src, dst, ins.at[i]).wait()

    fwd_raw, back_raw = fw[0, 0], bw[0, 0]
    fwd_norm = fwd_raw / jnp.sum(fwd_raw, axis=0, keepdims=True)
    back_norm = back_raw / jnp.sum(back_raw, axis=0, keepdims=True)
    fwd_place, back_place = fi[0, 0].astype(F32), bi[0, 0].astype(F32)
    present = om[0, 0].astype(F32)
    for g in range(SEQ):
        for tile in range(3):
            at = (g * 3 + tile) * TOK
            pks[g, tile * 4 : tile * 4 + 4, :] = fwd_place[:, at : at + TOK]
            pks[g, 12 + tile * 4 : 16 + tile * 4, :] = fwd_norm[:, at : at + TOK]
        at = g * TOK
        pks[g, 24:28, :] = back_place[:, at : at + TOK]
        pks[g, 28:32, :] = back_norm[:, at : at + TOK]
        pks[g, 32:34, :] = present[:, at : at + TOK]
        pks[g, 34:40, :] = jnp.zeros((6, TOK), F32)
    copy(pks.at[z], pk.at[2 + z], pr.at[edge])

    def send_pack(step, _):
        other = (z + step) % ROW
        send(pks.at[other], pk.at[2 + z], ps, pr.at[edge], along_view(first + other))
        return 0

    lax.fori_loop(1, ROW, send_pack, 0)

    for h in range(1, HERE):
        send_head(h, 0)
        send_head(h, 1)

    def head_sums(c, carry):
        at = pl.multiple_of(c * FEAT, FEAT)
        turned = hw[:, pl.ds(at, FEAT)].astype(F32)
        gained = jnp.sum(turned * gain[:, pl.ds(at, FEAT)], axis=1, keepdims=True)
        gsum[c] = jnp.broadcast_to(gained, (LAT, TOK))
        return carry + jnp.sum(turned * shift[:, pl.ds(at, FEAT)], axis=1, keepdims=True)

    shift_sum = lax.fori_loop(0, SEQ, head_sums, jnp.zeros((LAT, 1), F32))
    for h in range(HERE):
        at = pl.multiple_of((seq * HERE + h) * DH, DH)
        scaled = hw[:, pl.ds(at, DH)].astype(F32) * gain[:, pl.ds(at, DH)]
        wg[h] = jnp.concatenate(split(scaled), axis=0)
        hsum[h] = jnp.broadcast_to(jnp.sum(scaled, axis=1, keepdims=True), (LAT, TOK))
    diagonal = lax.broadcasted_iota(jnp.int32, (LAT, LAT), 0) == lax.broadcasted_iota(
        jnp.int32, (LAT, LAT), 1
    )
    mix_col = jnp.sum(
        jnp.where(diagonal, jnp.broadcast_to(mix[...], (LAT, LAT)), 0.0), axis=1, keepdims=True
    )
    cols[0] = jnp.broadcast_to(shift_sum, (LAT, TOK))
    cols[1] = jnp.broadcast_to(mix_col, (LAT, TOK))

    rate = math.log2(math.e) / math.sqrt(DH)

    def attend(h):
        for t, (_, dst) in enumerate(arrays):
            wait(dst.at[h], xr.at[t, h])

        vt[...] = vb[h].reshape(SEQ * TOK, DH).T

        def block(step, _):
            j = (step + 2 * (1 - z // 4)) % 4
            rows = qb[h, pl.ds(2 * j, 2)].reshape(2 * TOK, DH)
            scores = dot(kb[h].reshape(SEQ * TOK, DH), rows, ((1,), (1,)))
            highest = jnp.max(scores, axis=0, keepdims=True)
            probs = jnp.exp2((scores - highest) * rate)
            total = jnp.sum(probs, axis=0, keepdims=True)
            mixed = dot(vt[...], probs.astype(BF), ((1,), (0,)))
            mixed = (mixed / total).astype(BF)
            for half in range(2):
                g = 2 * j + half
                att[h, g] = mixed[:, half * TOK : (half + 1) * TOK]

                @pl.when(g != z)
                def _():
                    send(att.at[h, g], ext.at[h, 2 + z], zs.at[h], zr.at[h, edge], along_view(first + g))

                @pl.when(g == z)
                def _():
                    copy(att.at[h, g], ext.at[h, 2 + z], zr.at[h, edge])

            return 0

        lax.fori_loop(0, SEQ // 2, block, 0)

    def join(u, _):
        a0, a1 = pk[u + 1, 32:33, :], pk[u + 1, 33:34, :]
        share = 1.0 / (1.0 + a0 + a1)
        for i, factor in enumerate((a0 * share, share, a1 * share)):
            tile = 2 - i
            part = spread(
                pk[u + i, tile * 4 : tile * 4 + 4, :],
                pk[u + i, 12 + tile * 4 : 16 + tile * 4, :] * factor,
                TOK,
            )
            upper, lower = split(part)
            jt[u, i * TOK : (i + 1) * TOK, :] = upper
            jt[u, (3 + i) * TOK : (4 + i) * TOK, :] = lower
        return 0


    def compose(w, _):
        back = spread(pk[w + 2, 24:28, :], pk[w + 2, 28:32, :], 3 * TOK)
        parts = [jnp.zeros((TOK, TOK), F32) for _ in range(5)]
        for b in range(3):
            upper, lower = split(back[b * TOK : (b + 1) * TOK])
            wide = dot(jt[w + b], jnp.concatenate([upper, lower], axis=1), ((1,), (0,)))
            wide = wide[:, :TOK] + wide[:, TOK:]
            wide = wide[: 3 * TOK] + wide[3 * TOK :]
            for i in range(3):
                parts[b + i] = parts[b + i] + wide[i * TOK : (i + 1) * TOK]
        for i in range(5):
            upper, lower = split(parts[i])
            mt[w, i * TOK : (i + 1) * TOK, :TOK] = upper
            mt[w, i * TOK : (i + 1) * TOK, TOK:] = lower
        return 0

    attend(0)

    wait(pk.at[2:4], pr.at[0])
    wait(pk.at[8:10], pr.at[2])
    send(pk.at[8:10], pk.at[0:2], pys.at[0], pyr.at[0], along_view(nxt))
    send(pk.at[2:4], pk.at[10:12], pys.at[1], pyr.at[1], along_view(prv))

    attend(1)
    wait(pk.at[4:8], pr.at[1])
    wait(pk.at[0:2], pyr.at[0])
    wait(pk.at[10:12], pyr.at[1])
    lax.fori_loop(0, ROW + 2, join, 0)
    attend(2)
    lax.fori_loop(0, ROW, compose, 0)
    attend(3)

    def blend(h, low, high):
        def one(w, _):
            source = jnp.concatenate([ext[h, w + i] for i in range(5)], axis=1)
            wide = dot(source, mt[w], ((1,), (0,)))
            x = wide[:, :TOK] + wide[:, TOK:]
            mean = jnp.sum(x, axis=0, keepdims=True) * (1.0 / DH)
            centred = x - mean
            stats[w, h : h + 1, :] = mean
            stats[w, HERE + h : HERE + h + 1, :] = jnp.sum(centred * centred, axis=0, keepdims=True)
            wide = dot(wg[h], centred.astype(BF), ((1,), (0,)))
            part = wide[:LAT] + wide[LAT:]
            if h > 0:
                part = part + acc[w]
            if h < HERE - 1:
                acc[w] = part
                return 0

            means = stats[w, 0:HERE, :]
            mean = jnp.sum(means, axis=0, keepdims=True) * (1.0 / HERE)
            apart = means - mean
            squares = jnp.sum(stats[w, HERE:, :] + DH * apart * apart, axis=0, keepdims=True)
            for i in range(HERE):
                part = part + hsum[i] * apart[i : i + 1]
            rows = []
            for row in (mean, squares):
                for _ in range(3):
                    piece = row.astype(BF).astype(F32)
                    rows.append(piece)
                    row = row - piece
            rows.append(jnp.zeros((10, TOK), F32))
            sp[w, 0:LAT, :] = part.astype(BF)
            sp[w, LAT:, :] = jnp.concatenate(rows, axis=0).astype(BF)

            @pl.when(w != seq)
            def _():
                send(sp.at[w], rp.at[seq], rs, rr, along_seq(w))

            @pl.when(w == seq)
            def _():
                copy(sp.at[w], rp.at[seq], rr)

            return 0

        lax.fori_loop(low, high, one, 0)

    for h in range(HERE):
        wait(ext.at[h, 2:4], zr.at[h, 0])
        wait(ext.at[h, 8:10], zr.at[h, 2])
        send(ext.at[h, 8:10], ext.at[h, 0:2], ys.at[h, 0], yr.at[h, 0], along_view(nxt))
        send(ext.at[h, 2:4], ext.at[h, 10:12], ys.at[h, 1], yr.at[h, 1], along_view(prv))
        wait(ext.at[h, 4:8], zr.at[h, 1])
        blend(h, 2, 6)
        wait(ext.at[h, 0:2], yr.at[h, 0])
        blend(h, 0, 2)
        wait(ext.at[h, 10:12], yr.at[h, 1])
        blend(h, 6, 8)

    wait(rp, rr)
    pieces = rp[:, LAT:, :].astype(F32)
    means = pieces[:, 0] + pieces[:, 1] + pieces[:, 2]
    squares = pieces[:, 3] + pieces[:, 4] + pieces[:, 5]
    mean = jnp.sum(means, axis=0, keepdims=True) * (1.0 / SEQ)
    apart = means - mean
    squares = jnp.sum(squares + FEAT * apart * apart, axis=0, keepdims=True)
    deviation = jnp.sqrt(squares * (1.0 / (SEQ * FEAT)) + 1e-06)
    summed = jnp.zeros((LAT, TOK), F32)
    for i in range(SEQ):
        summed = summed + (rp[i, :LAT, :].astype(F32) + gsum[i] * apart[i : i + 1])
    velocity = summed / deviation + cols[0]
    vs[...] = velocity
    vsb[...] = velocity.astype(BF)
    send(vsb, voth, fs.at[1], fr.at[1], across)

    @pl.when(z != seq)
    def _():
        send(vs, vown, fs.at[0], fr.at[0], partner)

    @pl.when(z == seq)
    def _():
        copy(vs, vown, fr.at[0])

    wait(vown, fr.at[0])
    wait(voth, fr.at[1])
    mine = vown[...]
    out[0, 0] = lat[0, 0] - 0.8 * (mine + cols[1] * (voth[...].astype(F32) - mine))

    for h in range(HERE):
        for t, (_, dst) in enumerate(arrays):
            wait(dst.at[h, 0 : SEQ - 1], xs.at[t, h])
        wait(att.at[h, 0 : ROW - 1], zs.at[h])
        wait(ext.at[h, 8:10], ys.at[h, 0])
        wait(ext.at[h, 2:4], ys.at[h, 1])
    wait(pks.at[0 : ROW - 1], ps)
    wait(pk.at[8:10], pys.at[0])
    wait(pk.at[2:4], pys.at[1])
    wait(sp.at[0 : SEQ - 1], rs)
    wait(vsb, fs.at[1])

    @pl.when(z != seq)
    def _():
        wait(vs, fs.at[0])


def local(
    queries, keys, values, fwd_index, fwd_weight, own_map, back_index, back_weight,
    head_gain, head_shift, head_weight, latents, eye_mix,
):
    hbm = pl.BlockSpec(memory_space=pltpu.HBM)
    vmem = pl.BlockSpec(memory_space=pltpu.VMEM)
    dma = pltpu.SemaphoreType.DMA
    block = (TOK, DH)
    return pl.pallas_call(
        kernel,
        out_shape=jax.ShapeDtypeStruct((1, 1, LAT, TOK), F32),
        in_specs=[hbm] * 13,
        out_specs=vmem,
        scratch_shapes=[
            pltpu.VMEM(fwd_index.shape, jnp.int32),
            pltpu.VMEM(fwd_weight.shape, F32),
            pltpu.VMEM(own_map.shape, jnp.int32),
            pltpu.VMEM(back_index.shape, jnp.int32),
            pltpu.VMEM(back_weight.shape, F32),
            pltpu.VMEM((1, SEQ * FEAT), F32),
            pltpu.VMEM((1, SEQ * FEAT), F32),
            pltpu.VMEM((LAT, SEQ * FEAT), BF),
            pltpu.VMEM((1, 1, LAT, TOK), F32),
            pltpu.VMEM((1, LAT), F32),
            pltpu.VMEM((HERE, SEQ) + block, BF),
            pltpu.VMEM((HERE, SEQ) + block, BF),
            pltpu.VMEM((HERE, SEQ) + block, BF),
            pltpu.VMEM((HERE, SEQ) + block, BF),
            pltpu.VMEM((HERE, ROW + 4) + block, BF),
            pltpu.VMEM((SEQ, PACK, TOK), F32),
            pltpu.VMEM((ROW + 4, PACK, TOK), F32),
            pltpu.VMEM((DH, SEQ * TOK), BF),
            pltpu.VMEM((ROW + 2, 6 * TOK, TOK), BF),
            pltpu.VMEM((ROW, 5 * TOK, 2 * TOK), BF),
            pltpu.VMEM((ROW, LAT, TOK), F32),
            pltpu.VMEM((ROW, 2 * HERE, TOK), F32),
            pltpu.VMEM((HERE, 2 * LAT, DH), BF),
            pltpu.VMEM((SEQ, LAT, TOK), F32),
            pltpu.VMEM((HERE, LAT, TOK), F32),
            pltpu.VMEM((2, LAT, TOK), F32),
            pltpu.VMEM((ROW, LAT + 16, TOK), BF),
            pltpu.VMEM((SEQ, LAT + 16, TOK), BF),
            pltpu.VMEM((LAT, TOK), F32),
            pltpu.VMEM((LAT, TOK), BF),
            pltpu.VMEM((LAT, TOK), F32),
            pltpu.VMEM((LAT, TOK), BF),
            dma((10,)),
            dma((3, HERE)), dma((3, HERE)),
            dma((HERE,)), dma((HERE, 3)),
            dma((HERE, 2)), dma((HERE, 2)),
            dma(()), dma((3,)),
            dma((2,)), dma((2,)),
            dma(()), dma(()),
            dma((2,)), dma((2,)),
        ],
        compiler_params=pltpu.CompilerParams(
            collective_id=0, has_side_effects=True, vmem_limit_bytes=60 * 2**20
        ),
    )(
        queries, keys, values, fwd_index, fwd_weight, own_map, back_index, back_weight,
        head_gain.reshape(1, -1), head_shift.reshape(1, -1), head_weight.T, latents,
        eye_mix.reshape(1, -1),
    )


def solution(mesh):
    placed = (
        P("view", "eye", "seq", None),
        P("view", "eye", "seq", None),
        P("view", "eye", "seq", None),
        P("view", "eye", None, None),
        P("view", "eye", None, None),
        P("view", "eye", None, None),
        P("view", "eye", None, None),
        P("view", "eye", None, None),
        P(),
        P(),
        P(),
        P("view", "eye", None, "seq"),
        P(),
    )
    return jax.shard_map(
        local, mesh=mesh, in_specs=placed, out_specs=P("view", "eye", None, "seq"), check_vma=False
    )
```

```python
import math

import jax
import jax.numpy as jnp
from jax import lax
from jax.experimental import pallas as pl
from jax.experimental.pallas import tpu as pltpu
from jax.sharding import PartitionSpec as P

DH = 128
TOK = 128
SEQ = 8
ROW = 8
HERE = 4
FEAT = HERE * DH
LAT = 64
PACK = 40
MESH = pl.DeviceIdType.MESH
BF = jnp.bfloat16
F32 = jnp.float32


def dot(a, b, dims):
    return lax.dot_general(a, b, (dims, ((), ())), preferred_element_type=F32)


def split(x):
    upper = x.astype(BF)
    return upper, (x - upper.astype(F32)).astype(BF)


def wait(ref, sem):
    pltpu.make_async_copy(ref, ref, sem).wait()


def spread(index, weight, rows):
    places = lax.broadcasted_iota(jnp.int32, (rows, TOK), 0).astype(F32)
    total = jnp.zeros((rows, TOK), F32)
    for tap in range(4):
        total = total + jnp.where(places == index[tap : tap + 1], weight[tap : tap + 1], 0.0)
    return total


def kernel(
    q, k, v, fi_in, fw_in, om_in, bi_in, bw_in, gain_in, shift_in, hw_in, lat_in, mix_in, out,
    fi, fw, om, bi, bw, gain, shift, hw, lat, mix,
    kb, vb, qb, rb, att, ext, pks, pk, vt, jt, mt, acc, stats, wg, gsum, hsum, cols, sp, rp, vs, vsb, vown, voth,
    ins, xs, xr, bs, br, zs, zr, ys, yr, ps, pr, pys, pyr, rs, rr, fs, fr,
):
    view, eye, seq = lax.axis_index("view"), lax.axis_index("eye"), lax.axis_index("seq")
    row, z = view // ROW, view % ROW
    first = row * ROW
    edge = (z + 2) // 4
    nxt, prv = (view + ROW) % 32, (view + 32 - ROW) % 32
    partner = {"view": first + seq, "eye": eye, "seq": z}
    across = {"view": first + seq, "eye": 1 - eye, "seq": z}

    def along_seq(i):
        return {"view": view, "eye": eye, "seq": i}

    def along_view(i):
        return {"view": i, "eye": eye, "seq": seq}

    def send(src, dst, s, r, target):
        pltpu.make_async_remote_copy(
            src_ref=src, dst_ref=dst, send_sem=s, recv_sem=r, device_id=target, device_id_type=MESH
        ).start()

    def copy(src, dst, s):
        pltpu.make_async_copy(src, dst, s).start()

    small = (
        (fi_in, fi), (fw_in, fw), (om_in, om), (bi_in, bi), (bw_in, bw),
        (gain_in, gain), (shift_in, shift), (hw_in, hw), (lat_in, lat), (mix_in, mix),
    )
    for i, (src, dst) in enumerate(small):
        copy(src, dst, ins.at[i])

    barrier = pltpu.get_barrier_semaphore()

    def greet(target):
        pl.semaphore_signal(barrier, inc=1, device_id=target, device_id_type=MESH)

    for step in range(1, SEQ):
        greet(along_seq((seq + step) % SEQ))
        greet(along_view(first + (z + step) % ROW))
    greet(along_view(nxt))
    greet(along_view(prv))
    greet(across)

    @pl.when(z != seq)
    def _():
        greet(partner)

    pl.semaphore_wait(barrier, 2 * (SEQ - 1) + 3 + jnp.where(z == seq, 0, 1))

    chip, core = seq // 2, seq % 2
    opposite = (chip + 2) % 4 * 2
    target = (chip + 1 + 2 * core) % 4 * 2
    origin = (chip + 3 - 2 * core) % 4 * 2 + core
    arrays = ((k, kb), (v, vb), (q, qb))

    def block(src, other, h):
        start = pl.multiple_of((other * HERE + h) * DH, DH)
        return src.at[0, 0, :, pl.ds(start, DH)]

    def send_around(stage):
        h, side = stage // 2, stage % 2
        for t in range(2):
            src = block(arrays[t][0], opposite + side, h)
            send(src, rb.at[t, stage], xs.at[t, h], br.at[t, stage], along_seq(target + core))

    def hand_on(stage):
        h, side = stage // 2, stage % 2
        for t in range(2):
            wait(rb.at[t, stage], br.at[t, stage])
            send(rb.at[t, stage], arrays[t][1].at[h, origin], bs.at[t, stage], xr.at[t, h], along_seq(target + side))

    def send_stage(stage):
        h, side = stage // 2, stage % 2
        for t in (2, 0, 1):
            src, dst = arrays[t]

            def one(step, _):
                other = (chip + step) % 4 * 2 + side

                @pl.when(other != seq)
                def _():
                    send(block(src, other, h), dst.at[h, seq], xs.at[t, h], xr.at[t, h], along_seq(other))

                @pl.when(other == seq)
                def _():
                    copy(block(src, other, h), dst.at[h, seq], xr.at[t, h])

                return 0

            if t == 2:
                lax.fori_loop(1, 5, one, 0)
            else:
                lax.fori_loop(3, 6, one, 0)

    def advance(stage):
        hand_on(stage)
        if stage + 1 < 2 * HERE:
            send_stage(stage + 1)
        if stage + 2 < 2 * HERE:
            send_around(stage + 2)

    send_around(0)
    send_stage(0)
    send_around(1)

    for i, (src, dst) in enumerate(small):
        pltpu.make_async_copy(src, dst, ins.at[i]).wait()

    fwd_raw, back_raw = fw[0, 0], bw[0, 0]
    fwd_norm = fwd_raw / jnp.sum(fwd_raw, axis=0, keepdims=True)
    back_norm = back_raw / jnp.sum(back_raw, axis=0, keepdims=True)
    fwd_place, back_place = fi[0, 0].astype(F32), bi[0, 0].astype(F32)
    present = om[0, 0].astype(F32)
    for g in range(SEQ):
        for tile in range(3):
            at = (g * 3 + tile) * TOK
            pks[g, tile * 4 : tile * 4 + 4, :] = fwd_place[:, at : at + TOK]
            pks[g, 12 + tile * 4 : 16 + tile * 4, :] = fwd_norm[:, at : at + TOK]
        at = g * TOK
        pks[g, 24:28, :] = back_place[:, at : at + TOK]
        pks[g, 28:32, :] = back_norm[:, at : at + TOK]
        pks[g, 32:34, :] = present[:, at : at + TOK]
        pks[g, 34:40, :] = jnp.zeros((6, TOK), F32)
    copy(pks.at[z], pk.at[2 + z], pr.at[edge])

    def send_pack(step, _):
        other = (z + step) % ROW
        send(pks.at[other], pk.at[2 + z], ps, pr.at[edge], along_view(first + other))
        return 0

    lax.fori_loop(1, ROW, send_pack, 0)

    advance(0)

    def head_sums(c, carry):
        at = pl.multiple_of(c * FEAT, FEAT)
        turned = hw[:, pl.ds(at, FEAT)].astype(F32)
        gained = jnp.sum(turned * gain[:, pl.ds(at, FEAT)], axis=1, keepdims=True)
        gsum[c] = jnp.broadcast_to(gained, (LAT, TOK))
        return carry + jnp.sum(turned * shift[:, pl.ds(at, FEAT)], axis=1, keepdims=True)

    shift_sum = lax.fori_loop(0, SEQ, head_sums, jnp.zeros((LAT, 1), F32))
    for h in range(HERE):
        at = pl.multiple_of((seq * HERE + h) * DH, DH)
        scaled = hw[:, pl.ds(at, DH)].astype(F32) * gain[:, pl.ds(at, DH)]
        wg[h] = jnp.concatenate(split(scaled), axis=0)
        hsum[h] = jnp.broadcast_to(jnp.sum(scaled, axis=1, keepdims=True), (LAT, TOK))
    diagonal = lax.broadcasted_iota(jnp.int32, (LAT, LAT), 0) == lax.broadcasted_iota(
        jnp.int32, (LAT, LAT), 1
    )
    mix_col = jnp.sum(
        jnp.where(diagonal, jnp.broadcast_to(mix[...], (LAT, LAT)), 0.0), axis=1, keepdims=True
    )
    cols[0] = jnp.broadcast_to(shift_sum, (LAT, TOK))
    cols[1] = jnp.broadcast_to(mix_col, (LAT, TOK))

    rate = math.log2(math.e) / math.sqrt(DH)

    def attend(h):
        for t, (_, dst) in enumerate(arrays):
            wait(dst.at[h], xr.at[t, h])

        vt[...] = vb[h].reshape(SEQ * TOK, DH).T

        def rows_block(step, _):
            j = (step + 2 * (1 - z // 4)) % 4
            rows = qb[h, pl.ds(2 * j, 2)].reshape(2 * TOK, DH)
            scores = dot(kb[h].reshape(SEQ * TOK, DH), rows, ((1,), (1,)))
            highest = jnp.max(scores, axis=0, keepdims=True)
            probs = jnp.exp2((scores - highest) * rate)
            total = jnp.sum(probs, axis=0, keepdims=True)
            mixed = dot(vt[...], probs.astype(BF), ((1,), (0,)))
            mixed = (mixed / total).astype(BF)
            for half in range(2):
                g = 2 * j + half
                att[h, g] = mixed[:, half * TOK : (half + 1) * TOK]

                @pl.when(g != z)
                def _():
                    send(att.at[h, g], ext.at[h, 2 + z], zs.at[h], zr.at[h, edge], along_view(first + g))

                @pl.when(g == z)
                def _():
                    copy(att.at[h, g], ext.at[h, 2 + z], zr.at[h, edge])

            return 0

        lax.fori_loop(0, SEQ // 2, rows_block, 0)

    def join(u, _):
        a0, a1 = pk[u + 1, 32:33, :], pk[u + 1, 33:34, :]
        share = 1.0 / (1.0 + a0 + a1)
        for i, factor in enumerate((a0 * share, share, a1 * share)):
            tile = 2 - i
            part = spread(
                pk[u + i, tile * 4 : tile * 4 + 4, :],
                pk[u + i, 12 + tile * 4 : 16 + tile * 4, :] * factor,
                TOK,
            )
            upper, lower = split(part)
            jt[u, i * TOK : (i + 1) * TOK, :] = upper
            jt[u, (3 + i) * TOK : (4 + i) * TOK, :] = lower
        return 0


    def compose(w, _):
        back = spread(pk[w + 2, 24:28, :], pk[w + 2, 28:32, :], 3 * TOK)
        parts = [jnp.zeros((TOK, TOK), F32) for _ in range(5)]
        for b in range(3):
            upper, lower = split(back[b * TOK : (b + 1) * TOK])
            wide = dot(jt[w + b], jnp.concatenate([upper, lower], axis=1), ((1,), (0,)))
            wide = wide[:, :TOK] + wide[:, TOK:]
            wide = wide[: 3 * TOK] + wide[3 * TOK :]
            for i in range(3):
                parts[b + i] = parts[b + i] + wide[i * TOK : (i + 1) * TOK]
        for i in range(5):
            upper, lower = split(parts[i])
            mt[w, i * TOK : (i + 1) * TOK, :TOK] = upper
            mt[w, i * TOK : (i + 1) * TOK, TOK:] = lower
        return 0

    advance(1)
    attend(0)
    advance(2)

    wait(pk.at[2:4], pr.at[0])
    wait(pk.at[8:10], pr.at[2])
    send(pk.at[8:10], pk.at[0:2], pys.at[0], pyr.at[0], along_view(nxt))
    send(pk.at[2:4], pk.at[10:12], pys.at[1], pyr.at[1], along_view(prv))

    advance(3)
    attend(1)
    advance(4)
    wait(pk.at[4:8], pr.at[1])
    wait(pk.at[0:2], pyr.at[0])
    wait(pk.at[10:12], pyr.at[1])
    advance(5)
    lax.fori_loop(0, ROW + 2, join, 0)
    attend(2)
    advance(6)
    advance(7)
    lax.fori_loop(0, ROW, compose, 0)
    attend(3)

    def blend(h, low, high):
        def one(w, _):
            source = jnp.concatenate([ext[h, w + i] for i in range(5)], axis=1)
            wide = dot(source, mt[w], ((1,), (0,)))
            x = wide[:, :TOK] + wide[:, TOK:]
            mean = jnp.sum(x, axis=0, keepdims=True) * (1.0 / DH)
            centred = x - mean
            stats[w, h : h + 1, :] = mean
            stats[w, HERE + h : HERE + h + 1, :] = jnp.sum(centred * centred, axis=0, keepdims=True)
            wide = dot(wg[h], centred.astype(BF), ((1,), (0,)))
            part = wide[:LAT] + wide[LAT:]
            if h > 0:
                part = part + acc[w]
            if h < HERE - 1:
                acc[w] = part
                return 0

            means = stats[w, 0:HERE, :]
            mean = jnp.sum(means, axis=0, keepdims=True) * (1.0 / HERE)
            apart = means - mean
            squares = jnp.sum(stats[w, HERE:, :] + DH * apart * apart, axis=0, keepdims=True)
            for i in range(HERE):
                part = part + hsum[i] * apart[i : i + 1]
            rows = []
            for row in (mean, squares):
                for _ in range(3):
                    piece = row.astype(BF).astype(F32)
                    rows.append(piece)
                    row = row - piece
            rows.append(jnp.zeros((10, TOK), F32))
            sp[w, 0:LAT, :] = part.astype(BF)
            sp[w, LAT:, :] = jnp.concatenate(rows, axis=0).astype(BF)

            @pl.when(w != seq)
            def _():
                send(sp.at[w], rp.at[seq], rs, rr, along_seq(w))

            @pl.when(w == seq)
            def _():
                copy(sp.at[w], rp.at[seq], rr)

            return 0

        lax.fori_loop(low, high, one, 0)

    for h in range(HERE):
        wait(ext.at[h, 2:4], zr.at[h, 0])
        wait(ext.at[h, 8:10], zr.at[h, 2])
        send(ext.at[h, 8:10], ext.at[h, 0:2], ys.at[h, 0], yr.at[h, 0], along_view(nxt))
        send(ext.at[h, 2:4], ext.at[h, 10:12], ys.at[h, 1], yr.at[h, 1], along_view(prv))
        wait(ext.at[h, 4:8], zr.at[h, 1])
        blend(h, 2, 6)
        wait(ext.at[h, 0:2], yr.at[h, 0])
        blend(h, 0, 2)
        wait(ext.at[h, 10:12], yr.at[h, 1])
        blend(h, 6, 8)

    wait(rp, rr)
    pieces = rp[:, LAT:, :].astype(F32)
    means = pieces[:, 0] + pieces[:, 1] + pieces[:, 2]
    squares = pieces[:, 3] + pieces[:, 4] + pieces[:, 5]
    mean = jnp.sum(means, axis=0, keepdims=True) * (1.0 / SEQ)
    apart = means - mean
    squares = jnp.sum(squares + FEAT * apart * apart, axis=0, keepdims=True)
    deviation = jnp.sqrt(squares * (1.0 / (SEQ * FEAT)) + 1e-06)
    summed = jnp.zeros((LAT, TOK), F32)
    for i in range(SEQ):
        summed = summed + (rp[i, :LAT, :].astype(F32) + gsum[i] * apart[i : i + 1])
    velocity = summed / deviation + cols[0]
    vs[...] = velocity
    vsb[...] = velocity.astype(BF)
    send(vsb, voth, fs.at[1], fr.at[1], across)

    @pl.when(z != seq)
    def _():
        send(vs, vown, fs.at[0], fr.at[0], partner)

    @pl.when(z == seq)
    def _():
        copy(vs, vown, fr.at[0])

    wait(vown, fr.at[0])
    wait(voth, fr.at[1])
    mine = vown[...]
    out[0, 0] = lat[0, 0] - 0.8 * (mine + cols[1] * (voth[...].astype(F32) - mine))

    for h in range(HERE):
        for t, (_, dst) in enumerate(arrays):
            wait(dst.at[h, 0 : SEQ - 1], xs.at[t, h])
            if t < 2:
                for side in range(2):
                    wait(rb.at[t, 2 * h + side], bs.at[t, 2 * h + side])
        wait(att.at[h, 0 : ROW - 1], zs.at[h])
        wait(ext.at[h, 8:10], ys.at[h, 0])
        wait(ext.at[h, 2:4], ys.at[h, 1])
    wait(pks.at[0 : ROW - 1], ps)
    wait(pk.at[8:10], pys.at[0])
    wait(pk.at[2:4], pys.at[1])
    wait(sp.at[0 : SEQ - 1], rs)
    wait(vsb, fs.at[1])

    @pl.when(z != seq)
    def _():
        wait(vs, fs.at[0])


def local(
    queries, keys, values, fwd_index, fwd_weight, own_map, back_index, back_weight,
    head_gain, head_shift, head_weight, latents, eye_mix,
):
    hbm = pl.BlockSpec(memory_space=pltpu.HBM)
    vmem = pl.BlockSpec(memory_space=pltpu.VMEM)
    dma = pltpu.SemaphoreType.DMA
    block = (TOK, DH)
    return pl.pallas_call(
        kernel,
        out_shape=jax.ShapeDtypeStruct((1, 1, LAT, TOK), F32),
        in_specs=[hbm] * 13,
        out_specs=vmem,
        scratch_shapes=[
            pltpu.VMEM(fwd_index.shape, jnp.int32),
            pltpu.VMEM(fwd_weight.shape, F32),
            pltpu.VMEM(own_map.shape, jnp.int32),
            pltpu.VMEM(back_index.shape, jnp.int32),
            pltpu.VMEM(back_weight.shape, F32),
            pltpu.VMEM((1, SEQ * FEAT), F32),
            pltpu.VMEM((1, SEQ * FEAT), F32),
            pltpu.VMEM((LAT, SEQ * FEAT), BF),
            pltpu.VMEM((1, 1, LAT, TOK), F32),
            pltpu.VMEM((1, LAT), F32),
            pltpu.VMEM((HERE, SEQ) + block, BF),
            pltpu.VMEM((HERE, SEQ) + block, BF),
            pltpu.VMEM((HERE, SEQ) + block, BF),
            pltpu.VMEM((2, 2 * HERE) + block, BF),
            pltpu.VMEM((HERE, SEQ) + block, BF),
            pltpu.VMEM((HERE, ROW + 4) + block, BF),
            pltpu.VMEM((SEQ, PACK, TOK), F32),
            pltpu.VMEM((ROW + 4, PACK, TOK), F32),
            pltpu.VMEM((DH, SEQ * TOK), BF),
            pltpu.VMEM((ROW + 2, 6 * TOK, TOK), BF),
            pltpu.VMEM((ROW, 5 * TOK, 2 * TOK), BF),
            pltpu.VMEM((ROW, LAT, TOK), F32),
            pltpu.VMEM((ROW, 2 * HERE, TOK), F32),
            pltpu.VMEM((HERE, 2 * LAT, DH), BF),
            pltpu.VMEM((SEQ, LAT, TOK), F32),
            pltpu.VMEM((HERE, LAT, TOK), F32),
            pltpu.VMEM((2, LAT, TOK), F32),
            pltpu.VMEM((ROW, LAT + 16, TOK), BF),
            pltpu.VMEM((SEQ, LAT + 16, TOK), BF),
            pltpu.VMEM((LAT, TOK), F32),
            pltpu.VMEM((LAT, TOK), BF),
            pltpu.VMEM((LAT, TOK), F32),
            pltpu.VMEM((LAT, TOK), BF),
            dma((10,)),
            dma((3, HERE)), dma((3, HERE)),
            dma((2, 2 * HERE)), dma((2, 2 * HERE)),
            dma((HERE,)), dma((HERE, 3)),
            dma((HERE, 2)), dma((HERE, 2)),
            dma(()), dma((3,)),
            dma((2,)), dma((2,)),
            dma(()), dma(()),
            dma((2,)), dma((2,)),
        ],
        compiler_params=pltpu.CompilerParams(
            collective_id=0, has_side_effects=True, vmem_limit_bytes=60 * 2**20
        ),
    )(
        queries, keys, values, fwd_index, fwd_weight, own_map, back_index, back_weight,
        head_gain.reshape(1, -1), head_shift.reshape(1, -1), head_weight.T, latents,
        eye_mix.reshape(1, -1),
    )


def solution(mesh):
    placed = (
        P("view", "eye", "seq", None),
        P("view", "eye", "seq", None),
        P("view", "eye", "seq", None),
        P("view", "eye", None, None),
        P("view", "eye", None, None),
        P("view", "eye", None, None),
        P("view", "eye", None, None),
        P("view", "eye", None, None),
        P(),
        P(),
        P(),
        P("view", "eye", None, "seq"),
        P(),
    )
    return jax.shard_map(
        local, mesh=mesh, in_specs=placed, out_specs=P("view", "eye", None, "seq"), check_vma=False
    )
```

```python
import math

import jax
import jax.numpy as jnp
from jax import lax
from jax.experimental import pallas as pl
from jax.experimental.pallas import tpu as pltpu
from jax.sharding import PartitionSpec as P

DH = 128
TOK = 128
SEQ = 8
ROW = 8
HERE = 4
FEAT = HERE * DH
LAT = 64
PACK = 40
MESH = pl.DeviceIdType.MESH
BF = jnp.bfloat16
F32 = jnp.float32


def dot(a, b, dims):
    return lax.dot_general(a, b, (dims, ((), ())), preferred_element_type=F32)


def split(x):
    upper = x.astype(BF)
    return upper, (x - upper.astype(F32)).astype(BF)


def wait(ref, sem):
    pltpu.make_async_copy(ref, ref, sem).wait()


def spread(index, weight, rows):
    places = lax.broadcasted_iota(jnp.int32, (rows, TOK), 0).astype(F32)
    total = jnp.zeros((rows, TOK), F32)
    for tap in range(4):
        total = total + jnp.where(places == index[tap : tap + 1], weight[tap : tap + 1], 0.0)
    return total


def kernel(
    q, k, v, fi_in, fw_in, om_in, bi_in, bw_in, gain_in, shift_in, hw_in, lat_in, mix_in, out,
    fi, fw, om, bi, bw, gain, shift, hw, lat, mix,
    kvq, heads, rb, att, ext, pks, pk, vt, jt, mt, acc, stats, wg, gsum, hsum, cols, sp, rp, vs, vsb, vown, voth,
    ins, ks, xs, xr, bs, br, zs, zr, ys, yr, ps, pr, pys, pyr, rs, rr, fs, fr,
):
    view, eye, seq = lax.axis_index("view"), lax.axis_index("eye"), lax.axis_index("seq")
    row, z = view // ROW, view % ROW
    first = row * ROW
    edge = (z + 2) // 4
    nxt, prv = (view + ROW) % 32, (view + 32 - ROW) % 32
    partner = {"view": first + seq, "eye": eye, "seq": z}
    across = {"view": first + seq, "eye": 1 - eye, "seq": z}

    def along_seq(i):
        return {"view": view, "eye": eye, "seq": i}

    def along_view(i):
        return {"view": i, "eye": eye, "seq": seq}

    def send(src, dst, s, r, target):
        pltpu.make_async_remote_copy(
            src_ref=src, dst_ref=dst, send_sem=s, recv_sem=r, device_id=target, device_id_type=MESH
        ).start()

    def copy(src, dst, s):
        pltpu.make_async_copy(src, dst, s).start()

    small = (
        (fi_in, fi), (fw_in, fw), (om_in, om), (bi_in, bi), (bw_in, bw),
        (gain_in, gain), (shift_in, shift), (hw_in, hw), (lat_in, lat), (mix_in, mix),
    )
    for t, src in enumerate((k, v, q)):
        copy(src.at[0, 0], kvq.at[t], ks.at[t])
    for i, (src, dst) in enumerate(small):
        copy(src, dst, ins.at[i])

    barrier = pltpu.get_barrier_semaphore()

    def greet(target):
        pl.semaphore_signal(barrier, inc=1, device_id=target, device_id_type=MESH)

    for step in range(1, SEQ):
        greet(along_seq((seq + step) % SEQ))
        greet(along_view(first + (z + step) % ROW))
    greet(along_view(nxt))
    greet(along_view(prv))
    greet(across)

    @pl.when(z != seq)
    def _():
        greet(partner)

    pl.semaphore_wait(barrier, 2 * (SEQ - 1) + 3 + jnp.where(z == seq, 0, 1))

    chip, core = seq // 2, seq % 2
    opposite = (chip + 2) % 4 * 2
    target = (chip + 1 + 2 * core) % 4 * 2
    origin = (chip + 3 - 2 * core) % 4 * 2 + core

    def block(other, h):
        start = pl.multiple_of((other * HERE + h) * DH, DH)
        return kvq.at[:, :, pl.ds(start, DH)]

    def send_around(stage):
        h, side = stage // 2, stage % 2
        send(block(opposite + side, h), rb.at[stage], xs.at[h], br.at[stage], along_seq(target + core))

    def hand_on(stage):
        h, side = stage // 2, stage % 2
        wait(rb.at[stage], br.at[stage])
        send(rb.at[stage], heads.at[h, :, origin], bs.at[stage], xr.at[h], along_seq(target + side))

    def send_stage(stage):
        h, side = stage // 2, stage % 2
        for step in (1, 3):
            other = (chip + step) % 4 * 2 + side
            send(block(other, h), heads.at[h, :, seq], xs.at[h], xr.at[h], along_seq(other))
        other = chip * 2 + side

        @pl.when(core != side)
        def _():
            send(block(other, h), heads.at[h, :, seq], xs.at[h], xr.at[h], along_seq(other))

        @pl.when(core == side)
        def _():
            copy(block(other, h), heads.at[h, :, seq], xr.at[h])

    def advance(stage):
        hand_on(stage)
        if stage + 1 < 2 * HERE:
            send_stage(stage + 1)
        if stage + 2 < 2 * HERE:
            send_around(stage + 2)

    for t in range(3):
        wait(kvq.at[t], ks.at[t])
    send_around(0)
    send_stage(0)
    send_around(1)

    for i, (src, dst) in enumerate(small):
        pltpu.make_async_copy(src, dst, ins.at[i]).wait()

    fwd_raw, back_raw = fw[0, 0], bw[0, 0]
    fwd_norm = fwd_raw / jnp.sum(fwd_raw, axis=0, keepdims=True)
    back_norm = back_raw / jnp.sum(back_raw, axis=0, keepdims=True)
    fwd_place, back_place = fi[0, 0].astype(F32), bi[0, 0].astype(F32)
    present = om[0, 0].astype(F32)
    for g in range(SEQ):
        for tile in range(3):
            at = (g * 3 + tile) * TOK
            pks[g, tile * 4 : tile * 4 + 4, :] = fwd_place[:, at : at + TOK]
            pks[g, 12 + tile * 4 : 16 + tile * 4, :] = fwd_norm[:, at : at + TOK]
        at = g * TOK
        pks[g, 24:28, :] = back_place[:, at : at + TOK]
        pks[g, 28:32, :] = back_norm[:, at : at + TOK]
        pks[g, 32:34, :] = present[:, at : at + TOK]
        pks[g, 34:40, :] = jnp.zeros((6, TOK), F32)
    copy(pks.at[z], pk.at[2 + z], pr.at[edge])

    def send_pack(step, _):
        other = (z + step) % ROW
        send(pks.at[other], pk.at[2 + z], ps, pr.at[edge], along_view(first + other))
        return 0

    lax.fori_loop(1, ROW, send_pack, 0)

    advance(0)

    def head_sums(c, carry):
        at = pl.multiple_of(c * FEAT, FEAT)
        turned = hw[:, pl.ds(at, FEAT)].astype(F32)
        gained = jnp.sum(turned * gain[:, pl.ds(at, FEAT)], axis=1, keepdims=True)
        gsum[c] = jnp.broadcast_to(gained, (LAT, TOK))
        return carry + jnp.sum(turned * shift[:, pl.ds(at, FEAT)], axis=1, keepdims=True)

    shift_sum = lax.fori_loop(0, SEQ, head_sums, jnp.zeros((LAT, 1), F32))
    for h in range(HERE):
        at = pl.multiple_of((seq * HERE + h) * DH, DH)
        scaled = hw[:, pl.ds(at, DH)].astype(F32) * gain[:, pl.ds(at, DH)]
        wg[h] = jnp.concatenate(split(scaled), axis=0)
        hsum[h] = jnp.broadcast_to(jnp.sum(scaled, axis=1, keepdims=True), (LAT, TOK))
    diagonal = lax.broadcasted_iota(jnp.int32, (LAT, LAT), 0) == lax.broadcasted_iota(
        jnp.int32, (LAT, LAT), 1
    )
    mix_col = jnp.sum(
        jnp.where(diagonal, jnp.broadcast_to(mix[...], (LAT, LAT)), 0.0), axis=1, keepdims=True
    )
    cols[0] = jnp.broadcast_to(shift_sum, (LAT, TOK))
    cols[1] = jnp.broadcast_to(mix_col, (LAT, TOK))

    rate = math.log2(math.e) / math.sqrt(DH)

    def attend(h):
        wait(heads.at[h], xr.at[h])
        vt[...] = heads[h, 1].reshape(SEQ * TOK, DH).T

        def rows_block(step, _):
            groups = [(z + 1 + 2 * step + half) % SEQ for half in range(2)]
            rows = jnp.concatenate([heads[h, 2, g] for g in groups], axis=0)
            scores = dot(heads[h, 0].reshape(SEQ * TOK, DH), rows, ((1,), (1,)))
            highest = jnp.max(scores, axis=0, keepdims=True)
            probs = jnp.exp2((scores - highest) * rate)
            total = jnp.sum(probs, axis=0, keepdims=True)
            mixed = dot(vt[...], probs.astype(BF), ((1,), (0,)))
            mixed = (mixed / total).astype(BF)
            for half, g in enumerate(groups):
                att[h, g] = mixed[:, half * TOK : (half + 1) * TOK]

                @pl.when(g != z)
                def _():
                    send(att.at[h, g], ext.at[h, 2 + z], zs.at[h], zr.at[h, edge], along_view(first + g))

                @pl.when(g == z)
                def _():
                    copy(att.at[h, g], ext.at[h, 2 + z], zr.at[h, edge])

            return 0

        lax.fori_loop(0, SEQ // 2, rows_block, 0)

    def join(u, _):
        a0, a1 = pk[u + 1, 32:33, :], pk[u + 1, 33:34, :]
        share = 1.0 / (1.0 + a0 + a1)
        for i, factor in enumerate((a0 * share, share, a1 * share)):
            tile = 2 - i
            part = spread(
                pk[u + i, tile * 4 : tile * 4 + 4, :],
                pk[u + i, 12 + tile * 4 : 16 + tile * 4, :] * factor,
                TOK,
            )
            upper, lower = split(part)
            jt[u, i * TOK : (i + 1) * TOK, :] = upper
            jt[u, (3 + i) * TOK : (4 + i) * TOK, :] = lower
        return 0


    def compose(w, _):
        back = spread(pk[w + 2, 24:28, :], pk[w + 2, 28:32, :], 3 * TOK)
        parts = [jnp.zeros((TOK, TOK), F32) for _ in range(5)]
        for b in range(3):
            upper, lower = split(back[b * TOK : (b + 1) * TOK])
            wide = dot(jt[w + b], jnp.concatenate([upper, lower], axis=1), ((1,), (0,)))
            wide = wide[:, :TOK] + wide[:, TOK:]
            wide = wide[: 3 * TOK] + wide[3 * TOK :]
            for i in range(3):
                parts[b + i] = parts[b + i] + wide[i * TOK : (i + 1) * TOK]
        for i in range(5):
            upper, lower = split(parts[i])
            mt[w, i * TOK : (i + 1) * TOK, :TOK] = upper
            mt[w, i * TOK : (i + 1) * TOK, TOK:] = lower
        return 0

    advance(1)
    attend(0)
    advance(2)

    wait(pk.at[2:4], pr.at[0])
    wait(pk.at[8:10], pr.at[2])
    send(pk.at[8:10], pk.at[0:2], pys.at[0], pyr.at[0], along_view(nxt))
    send(pk.at[2:4], pk.at[10:12], pys.at[1], pyr.at[1], along_view(prv))

    advance(3)
    attend(1)
    advance(4)
    wait(pk.at[4:8], pr.at[1])
    wait(pk.at[0:2], pyr.at[0])
    wait(pk.at[10:12], pyr.at[1])
    advance(5)
    lax.fori_loop(0, ROW + 2, join, 0)
    attend(2)
    advance(6)
    advance(7)
    lax.fori_loop(0, ROW, compose, 0)
    attend(3)

    def blend(h, low, high):
        def one(w, _):
            source = jnp.concatenate([ext[h, w + i] for i in range(5)], axis=1)
            wide = dot(source, mt[w], ((1,), (0,)))
            x = wide[:, :TOK] + wide[:, TOK:]
            mean = jnp.sum(x, axis=0, keepdims=True) * (1.0 / DH)
            centred = x - mean
            stats[w, h : h + 1, :] = mean
            stats[w, HERE + h : HERE + h + 1, :] = jnp.sum(centred * centred, axis=0, keepdims=True)
            wide = dot(wg[h], centred.astype(BF), ((1,), (0,)))
            part = wide[:LAT] + wide[LAT:]
            if h > 0:
                part = part + acc[w]
            if h < HERE - 1:
                acc[w] = part
                return 0

            means = stats[w, 0:HERE, :]
            mean = jnp.sum(means, axis=0, keepdims=True) * (1.0 / HERE)
            apart = means - mean
            squares = jnp.sum(stats[w, HERE:, :] + DH * apart * apart, axis=0, keepdims=True)
            for i in range(HERE):
                part = part + hsum[i] * apart[i : i + 1]
            rows = []
            for row in (mean, squares):
                for _ in range(3):
                    piece = row.astype(BF).astype(F32)
                    rows.append(piece)
                    row = row - piece
            rows.append(jnp.zeros((10, TOK), F32))
            sp[w, 0:LAT, :] = part.astype(BF)
            sp[w, LAT:, :] = jnp.concatenate(rows, axis=0).astype(BF)

            @pl.when(w != seq)
            def _():
                send(sp.at[w], rp.at[seq], rs, rr, along_seq(w))

            @pl.when(w == seq)
            def _():
                copy(sp.at[w], rp.at[seq], rr)

            return 0

        lax.fori_loop(low, high, one, 0)

    for h in range(HERE):
        wait(ext.at[h, 2:4], zr.at[h, 0])
        wait(ext.at[h, 8:10], zr.at[h, 2])
        send(ext.at[h, 8:10], ext.at[h, 0:2], ys.at[h, 0], yr.at[h, 0], along_view(nxt))
        send(ext.at[h, 2:4], ext.at[h, 10:12], ys.at[h, 1], yr.at[h, 1], along_view(prv))
        wait(ext.at[h, 4:8], zr.at[h, 1])
        blend(h, 2, 6)
        wait(ext.at[h, 0:2], yr.at[h, 0])
        blend(h, 0, 2)
        wait(ext.at[h, 10:12], yr.at[h, 1])
        blend(h, 6, 8)

    wait(rp, rr)
    pieces = rp[:, LAT:, :].astype(F32)
    means = pieces[:, 0] + pieces[:, 1] + pieces[:, 2]
    squares = pieces[:, 3] + pieces[:, 4] + pieces[:, 5]
    mean = jnp.sum(means, axis=0, keepdims=True) * (1.0 / SEQ)
    apart = means - mean
    squares = jnp.sum(squares + FEAT * apart * apart, axis=0, keepdims=True)
    deviation = jnp.sqrt(squares * (1.0 / (SEQ * FEAT)) + 1e-06)
    summed = jnp.zeros((LAT, TOK), F32)
    for i in range(SEQ):
        summed = summed + (rp[i, :LAT, :].astype(F32) + gsum[i] * apart[i : i + 1])
    velocity = summed / deviation + cols[0]
    vs[...] = velocity
    vsb[...] = velocity.astype(BF)
    send(vsb, voth, fs.at[1], fr.at[1], across)

    @pl.when(z != seq)
    def _():
        send(vs, vown, fs.at[0], fr.at[0], partner)

    @pl.when(z == seq)
    def _():
        copy(vs, vown, fr.at[0])

    wait(vown, fr.at[0])
    wait(voth, fr.at[1])
    mine = vown[...]
    out[0, 0] = lat[0, 0] - 0.8 * (mine + cols[1] * (voth[...].astype(F32) - mine))

    for h in range(HERE):
        wait(heads.at[h, :, 0 : SEQ - 1], xs.at[h])
        for side in range(2):
            wait(rb.at[2 * h + side], bs.at[2 * h + side])
        wait(att.at[h, 0 : ROW - 1], zs.at[h])
        wait(ext.at[h, 8:10], ys.at[h, 0])
        wait(ext.at[h, 2:4], ys.at[h, 1])
    wait(pks.at[0 : ROW - 1], ps)
    wait(pk.at[8:10], pys.at[0])
    wait(pk.at[2:4], pys.at[1])
    wait(sp.at[0 : SEQ - 1], rs)
    wait(vsb, fs.at[1])

    @pl.when(z != seq)
    def _():
        wait(vs, fs.at[0])


def local(
    queries, keys, values, fwd_index, fwd_weight, own_map, back_index, back_weight,
    head_gain, head_shift, head_weight, latents, eye_mix,
):
    hbm = pl.BlockSpec(memory_space=pltpu.HBM)
    vmem = pl.BlockSpec(memory_space=pltpu.VMEM)
    dma = pltpu.SemaphoreType.DMA
    block = (TOK, DH)
    return pl.pallas_call(
        kernel,
        out_shape=jax.ShapeDtypeStruct((1, 1, LAT, TOK), F32),
        in_specs=[hbm] * 13,
        out_specs=vmem,
        scratch_shapes=[
            pltpu.VMEM(fwd_index.shape, jnp.int32),
            pltpu.VMEM(fwd_weight.shape, F32),
            pltpu.VMEM(own_map.shape, jnp.int32),
            pltpu.VMEM(back_index.shape, jnp.int32),
            pltpu.VMEM(back_weight.shape, F32),
            pltpu.VMEM((1, SEQ * FEAT), F32),
            pltpu.VMEM((1, SEQ * FEAT), F32),
            pltpu.VMEM((LAT, SEQ * FEAT), BF),
            pltpu.VMEM((1, 1, LAT, TOK), F32),
            pltpu.VMEM((1, LAT), F32),
            pltpu.VMEM((3, TOK, SEQ * FEAT), BF),
            pltpu.VMEM((HERE, 3, SEQ) + block, BF),
            pltpu.VMEM((2 * HERE, 3) + block, BF),
            pltpu.VMEM((HERE, SEQ) + block, BF),
            pltpu.VMEM((HERE, ROW + 4) + block, BF),
            pltpu.VMEM((SEQ, PACK, TOK), F32),
            pltpu.VMEM((ROW + 4, PACK, TOK), F32),
            pltpu.VMEM((DH, SEQ * TOK), BF),
            pltpu.VMEM((ROW + 2, 6 * TOK, TOK), BF),
            pltpu.VMEM((ROW, 5 * TOK, 2 * TOK), BF),
            pltpu.VMEM((ROW, LAT, TOK), F32),
            pltpu.VMEM((ROW, 2 * HERE, TOK), F32),
            pltpu.VMEM((HERE, 2 * LAT, DH), BF),
            pltpu.VMEM((SEQ, LAT, TOK), F32),
            pltpu.VMEM((HERE, LAT, TOK), F32),
            pltpu.VMEM((2, LAT, TOK), F32),
            pltpu.VMEM((ROW, LAT + 16, TOK), BF),
            pltpu.VMEM((SEQ, LAT + 16, TOK), BF),
            pltpu.VMEM((LAT, TOK), F32),
            pltpu.VMEM((LAT, TOK), BF),
            pltpu.VMEM((LAT, TOK), F32),
            pltpu.VMEM((LAT, TOK), BF),
            dma((10,)),
            dma((3,)),
            dma((HERE,)), dma((HERE,)),
            dma((2 * HERE,)), dma((2 * HERE,)),
            dma((HERE,)), dma((HERE, 3)),
            dma((HERE, 2)), dma((HERE, 2)),
            dma(()), dma((3,)),
            dma((2,)), dma((2,)),
            dma(()), dma(()),
            dma((2,)), dma((2,)),
        ],
        compiler_params=pltpu.CompilerParams(
            collective_id=0, has_side_effects=True, vmem_limit_bytes=60 * 2**20
        ),
    )(
        queries, keys, values, fwd_index, fwd_weight, own_map, back_index, back_weight,
        head_gain.reshape(1, -1), head_shift.reshape(1, -1), head_weight.T, latents,
        eye_mix.reshape(1, -1),
    )


def solution(mesh):
    placed = (
        P("view", "eye", "seq", None),
        P("view", "eye", "seq", None),
        P("view", "eye", "seq", None),
        P("view", "eye", None, None),
        P("view", "eye", None, None),
        P("view", "eye", None, None),
        P("view", "eye", None, None),
        P("view", "eye", None, None),
        P(),
        P(),
        P(),
        P("view", "eye", None, "seq"),
        P(),
    )
    return jax.shard_map(
        local, mesh=mesh, in_specs=placed, out_specs=P("view", "eye", None, "seq"), check_vma=False
    )
```

```python
import math

import jax
import jax.numpy as jnp
from jax import lax
from jax.experimental import pallas as pl
from jax.experimental.pallas import tpu as pltpu
from jax.sharding import PartitionSpec as P

DH = 128
TOK = 128
SEQ = 8
ROW = 8
HERE = 4
FEAT = HERE * DH
LAT = 64
PACK = 40
MESH = pl.DeviceIdType.MESH
BF = jnp.bfloat16
F32 = jnp.float32


def dot(a, b, dims):
    return lax.dot_general(a, b, (dims, ((), ())), preferred_element_type=F32)


def split(x):
    upper = x.astype(BF)
    return upper, (x - upper.astype(F32)).astype(BF)


def wait(ref, sem):
    pltpu.make_async_copy(ref, ref, sem).wait()


def spread(index, weight, rows):
    places = lax.broadcasted_iota(jnp.int32, (rows, TOK), 0).astype(F32)
    total = jnp.zeros((rows, TOK), F32)
    for tap in range(4):
        total = total + jnp.where(places == index[tap : tap + 1], weight[tap : tap + 1], 0.0)
    return total


def kernel(
    q, k, v, fi_in, fw_in, om_in, bi_in, bw_in, gain_in, shift_in, hw_in, lat_in, mix_in, out,
    fi, fw, om, bi, bw, gain, shift, hw, lat, mix,
    kvq, heads, rb, att, ext, pks, pk, vt, jt, mt, acc, stats, wg, gsum, hsum, cols, sp, rp, vs, vsb, vown, voth,
    ins, ks, xs, xr, bs, br, zs, zr, ys, yr, ps, pr, pys, pyr, rs, rr, fs, fr,
):
    view, eye, seq = lax.axis_index("view"), lax.axis_index("eye"), lax.axis_index("seq")
    row, z = view // ROW, view % ROW
    first = row * ROW
    edge = (z + 2) // 4
    nxt, prv = (view + ROW) % 32, (view + 32 - ROW) % 32
    partner = {"view": first + seq, "eye": eye, "seq": z}
    across = {"view": first + seq, "eye": 1 - eye, "seq": z}

    def along_seq(i):
        return {"view": view, "eye": eye, "seq": i}

    def along_view(i):
        return {"view": i, "eye": eye, "seq": seq}

    def send(src, dst, s, r, target):
        pltpu.make_async_remote_copy(
            src_ref=src, dst_ref=dst, send_sem=s, recv_sem=r, device_id=target, device_id_type=MESH
        ).start()

    def copy(src, dst, s):
        pltpu.make_async_copy(src, dst, s).start()

    small = (
        (fi_in, fi), (fw_in, fw), (om_in, om), (bi_in, bi), (bw_in, bw),
        (gain_in, gain), (shift_in, shift), (hw_in, hw), (lat_in, lat), (mix_in, mix),
    )
    for t, src in enumerate((k, v, q)):
        copy(src.at[0, 0], kvq.at[t], ks.at[t])
    for i, (src, dst) in enumerate(small):
        copy(src, dst, ins.at[i])

    barrier = pltpu.get_barrier_semaphore()

    def greet(target):
        pl.semaphore_signal(barrier, inc=1, device_id=target, device_id_type=MESH)

    for step in range(1, SEQ):
        greet(along_seq((seq + step) % SEQ))
        greet(along_view(first + (z + step) % ROW))
    greet(along_view(nxt))
    greet(along_view(prv))
    greet(across)

    @pl.when(z != seq)
    def _():
        greet(partner)

    pl.semaphore_wait(barrier, 2 * (SEQ - 1) + 3 + jnp.where(z == seq, 0, 1))

    chip, core = seq // 2, seq % 2
    opposite = (chip + 2) % 4 * 2
    target = (chip + 1 + 2 * core) % 4 * 2
    origin = (chip + 3 - 2 * core) % 4 * 2 + core

    def block(other, h):
        start = pl.multiple_of((other * HERE + h) * DH, DH)
        return kvq.at[:, :, pl.ds(start, DH)]

    def send_around(stage):
        h, side = stage // 2, stage % 2
        send(block(opposite + side, h), rb.at[stage], xs.at[h], br.at[stage], along_seq(target + core))

    def hand_on(stage):
        h, side = stage // 2, stage % 2
        wait(rb.at[stage], br.at[stage])
        send(rb.at[stage], heads.at[h, :, origin], bs.at[stage], xr.at[h], along_seq(target + side))

    def send_stage(stage):
        h, side = stage // 2, stage % 2
        for step in (1, 3):
            other = (chip + step) % 4 * 2 + side
            send(block(other, h), heads.at[h, :, seq], xs.at[h], xr.at[h], along_seq(other))
        other = chip * 2 + side

        @pl.when(core != side)
        def _():
            send(block(other, h), heads.at[h, :, seq], xs.at[h], xr.at[h], along_seq(other))

        @pl.when(core == side)
        def _():
            copy(block(other, h), heads.at[h, :, seq], xr.at[h])

    def advance(stage):
        hand_on(stage)
        if stage + 1 < 2 * HERE:
            send_stage(stage + 1)
        if stage + 2 < 2 * HERE:
            send_around(stage + 2)

    for t in range(3):
        wait(kvq.at[t], ks.at[t])
    send_around(0)
    send_stage(0)
    send_around(1)

    for i, (src, dst) in enumerate(small):
        pltpu.make_async_copy(src, dst, ins.at[i]).wait()

    fwd_raw, back_raw = fw[0, 0], bw[0, 0]
    fwd_norm = fwd_raw / jnp.sum(fwd_raw, axis=0, keepdims=True)
    back_norm = back_raw / jnp.sum(back_raw, axis=0, keepdims=True)
    fwd_place, back_place = fi[0, 0].astype(F32), bi[0, 0].astype(F32)
    present = om[0, 0].astype(F32)
    for g in range(SEQ):
        for tile in range(3):
            at = (g * 3 + tile) * TOK
            pks[g, tile * 4 : tile * 4 + 4, :] = fwd_place[:, at : at + TOK]
            pks[g, 12 + tile * 4 : 16 + tile * 4, :] = fwd_norm[:, at : at + TOK]
        at = g * TOK
        pks[g, 24:28, :] = back_place[:, at : at + TOK]
        pks[g, 28:32, :] = back_norm[:, at : at + TOK]
        pks[g, 32:34, :] = present[:, at : at + TOK]
        pks[g, 34:40, :] = jnp.zeros((6, TOK), F32)
    copy(pks.at[z], pk.at[2 + z], pr.at[edge])

    def send_pack(step, _):
        other = (z + step) % ROW
        send(pks.at[other], pk.at[2 + z], ps, pr.at[edge], along_view(first + other))
        return 0

    lax.fori_loop(1, ROW, send_pack, 0)

    advance(0)

    def head_sums(c, carry):
        at = pl.multiple_of(c * FEAT, FEAT)
        turned = hw[:, pl.ds(at, FEAT)].astype(F32)
        gained = jnp.sum(turned * gain[:, pl.ds(at, FEAT)], axis=1, keepdims=True)
        gsum[c] = jnp.broadcast_to(gained, (LAT, TOK))
        return carry + jnp.sum(turned * shift[:, pl.ds(at, FEAT)], axis=1, keepdims=True)

    shift_sum = lax.fori_loop(0, SEQ, head_sums, jnp.zeros((LAT, 1), F32))
    for h in range(HERE):
        at = pl.multiple_of((seq * HERE + h) * DH, DH)
        scaled = hw[:, pl.ds(at, DH)].astype(F32) * gain[:, pl.ds(at, DH)]
        wg[h] = jnp.concatenate(split(scaled), axis=0)
        hsum[h] = jnp.broadcast_to(jnp.sum(scaled, axis=1, keepdims=True), (LAT, TOK))
    diagonal = lax.broadcasted_iota(jnp.int32, (LAT, LAT), 0) == lax.broadcasted_iota(
        jnp.int32, (LAT, LAT), 1
    )
    mix_col = jnp.sum(
        jnp.where(diagonal, jnp.broadcast_to(mix[...], (LAT, LAT)), 0.0), axis=1, keepdims=True
    )
    cols[0] = jnp.broadcast_to(shift_sum, (LAT, TOK))
    cols[1] = jnp.broadcast_to(mix_col, (LAT, TOK))

    rate = math.log2(math.e) / math.sqrt(DH)

    def attend(h):
        wait(heads.at[h], xr.at[h])
        vt[...] = heads[h, 1].reshape(SEQ * TOK, DH).T

        def query_blocks(step, _):
            groups = [(z + 1 + 4 * step + i) % SEQ for i in range(4)]
            keyed = heads[h, 0].reshape(SEQ * TOK, DH)
            rows = [jnp.concatenate([heads[h, 2, g] for g in groups[i : i + 2]], axis=0) for i in (0, 2)]
            scores = [dot(keyed, r, ((1,), (1,))) for r in rows]
            highest = [jnp.max(x, axis=0, keepdims=True) for x in scores]
            probs = [jnp.exp2((x - m) * rate) for x, m in zip(scores, highest)]
            total = [jnp.sum(p, axis=0, keepdims=True) for p in probs]
            mixed = [dot(vt[...], p.astype(BF), ((1,), (0,))) for p in probs]
            mixed = [(m / t).astype(BF) for m, t in zip(mixed, total)]
            for i, g in enumerate(groups):
                att[h, g] = mixed[i // 2][:, i % 2 * TOK : (i % 2 + 1) * TOK]
            for g in groups[:3]:
                send(att.at[h, g], ext.at[h, 2 + z], zs.at[h], zr.at[h, edge], along_view(first + g))
            g = groups[3]

            @pl.when(step == 0)
            def _():
                send(att.at[h, g], ext.at[h, 2 + z], zs.at[h], zr.at[h, edge], along_view(first + g))

            @pl.when(step == 1)
            def _():
                copy(att.at[h, g], ext.at[h, 2 + z], zr.at[h, edge])

            return 0

        lax.fori_loop(0, 2, query_blocks, 0)

    def join(u):
        a0, a1 = pk[u + 1, 32:33, :], pk[u + 1, 33:34, :]
        share = 1.0 / (1.0 + a0 + a1)
        for i, factor in enumerate((a0 * share, share, a1 * share)):
            tile = 2 - i
            part = spread(
                pk[u + i, tile * 4 : tile * 4 + 4, :],
                pk[u + i, 12 + tile * 4 : 16 + tile * 4, :] * factor,
                TOK,
            )
            upper, lower = split(part)
            jt[u, i * TOK : (i + 1) * TOK, :] = upper
            jt[u, (3 + i) * TOK : (4 + i) * TOK, :] = lower


    def compose(w):
        back = spread(pk[w + 2, 24:28, :], pk[w + 2, 28:32, :], 3 * TOK)
        parts = [jnp.zeros((TOK, TOK), F32) for _ in range(5)]
        for b in range(3):
            upper, lower = split(back[b * TOK : (b + 1) * TOK])
            wide = dot(jt[w + b], jnp.concatenate([upper, lower], axis=1), ((1,), (0,)))
            wide = wide[:, :TOK] + wide[:, TOK:]
            wide = wide[: 3 * TOK] + wide[3 * TOK :]
            for i in range(3):
                parts[b + i] = parts[b + i] + wide[i * TOK : (i + 1) * TOK]
        for i in range(5):
            upper, lower = split(parts[i])
            mt[w, i * TOK : (i + 1) * TOK, :TOK] = upper
            mt[w, i * TOK : (i + 1) * TOK, TOK:] = lower

    def in_pairs(count, step):
        def two(i, _):
            step(2 * i)
            step(2 * i + 1)
            return 0

        lax.fori_loop(0, count // 2, two, 0)

    def blend(h, views):
        wide = [
            dot(jnp.concatenate([ext[h, w + i] for i in range(5)], axis=1), mt[w], ((1,), (0,)))
            for w in views
        ]
        x = [a[:, :TOK] + a[:, TOK:] for a in wide]
        mean = [jnp.sum(a, axis=0, keepdims=True) * (1.0 / DH) for a in x]
        centred = [a - m for a, m in zip(x, mean)]
        squares = [jnp.sum(a * a, axis=0, keepdims=True) for a in centred]
        wide = dot(wg[h], jnp.concatenate([a.astype(BF) for a in centred], axis=1), ((1,), (0,)))
        wide = wide[:LAT] + wide[LAT:]
        part = [wide[:, i * TOK : (i + 1) * TOK] for i in range(len(views))]
        if h > 0:
            part = [a + acc[w] for a, w in zip(part, views)]
        for a, m, w in zip(squares, mean, views):
            stats[w, h : h + 1, :] = m
            stats[w, HERE + h : HERE + h + 1, :] = a
        if h < HERE - 1:
            for a, w in zip(part, views):
                acc[w] = a
            return

        for part_here, w in zip(part, views):
            means = stats[w, 0:HERE, :]
            middle = jnp.sum(means, axis=0, keepdims=True) * (1.0 / HERE)
            apart = means - middle
            summed = jnp.sum(stats[w, HERE:, :] + DH * apart * apart, axis=0, keepdims=True)
            for i in range(HERE):
                part_here = part_here + hsum[i] * apart[i : i + 1]
            rows = []
            for line in (middle, summed):
                for _ in range(3):
                    piece = line.astype(BF).astype(F32)
                    rows.append(piece)
                    line = line - piece
            rows.append(jnp.zeros((10, TOK), F32))
            sp[w, 0:LAT, :] = part_here.astype(BF)
            sp[w, LAT:, :] = jnp.concatenate(rows, axis=0).astype(BF)
        for w in views:

            @pl.when(w != seq)
            def _():
                send(sp.at[w], rp.at[seq], rs, rr, along_seq(w))

            @pl.when(w == seq)
            def _():
                copy(sp.at[w], rp.at[seq], rr)

    def forward(h):
        wait(ext.at[h, 2:4], zr.at[h, 0])
        wait(ext.at[h, 8:10], zr.at[h, 2])
        send(ext.at[h, 8:10], ext.at[h, 0:2], ys.at[h, 0], yr.at[h, 0], along_view(nxt))
        send(ext.at[h, 2:4], ext.at[h, 10:12], ys.at[h, 1], yr.at[h, 1], along_view(prv))

    def finish(h):
        wait(ext.at[h, 4:8], zr.at[h, 1])
        blend(h, (2, 3, 4, 5))
        wait(ext.at[h, 0:2], yr.at[h, 0])
        wait(ext.at[h, 10:12], yr.at[h, 1])
        blend(h, (0, 1, 6, 7))

    advance(1)
    attend(0)
    advance(2)

    wait(pk.at[2:4], pr.at[0])
    wait(pk.at[8:10], pr.at[2])
    send(pk.at[8:10], pk.at[0:2], pys.at[0], pyr.at[0], along_view(nxt))
    send(pk.at[2:4], pk.at[10:12], pys.at[1], pyr.at[1], along_view(prv))

    advance(3)
    attend(1)
    advance(4)
    wait(pk.at[4:8], pr.at[1])
    wait(pk.at[0:2], pyr.at[0])
    wait(pk.at[10:12], pyr.at[1])
    advance(5)
    in_pairs(ROW + 2, join)
    attend(2)
    advance(6)
    advance(7)
    in_pairs(ROW, compose)
    forward(0)
    finish(0)
    forward(1)
    attend(3)
    forward(2)
    finish(1)
    finish(2)
    forward(3)
    finish(3)
    wait(rp, rr)
    pieces = rp[:, LAT:, :].astype(F32)
    means = pieces[:, 0] + pieces[:, 1] + pieces[:, 2]
    squares = pieces[:, 3] + pieces[:, 4] + pieces[:, 5]
    mean = jnp.sum(means, axis=0, keepdims=True) * (1.0 / SEQ)
    apart = means - mean
    squares = jnp.sum(squares + FEAT * apart * apart, axis=0, keepdims=True)
    deviation = jnp.sqrt(squares * (1.0 / (SEQ * FEAT)) + 1e-06)
    summed = jnp.zeros((LAT, TOK), F32)
    for i in range(SEQ):
        summed = summed + (rp[i, :LAT, :].astype(F32) + gsum[i] * apart[i : i + 1])
    velocity = summed / deviation + cols[0]
    vs[...] = velocity
    vsb[...] = velocity.astype(BF)
    send(vsb, voth, fs.at[1], fr.at[1], across)

    @pl.when(z != seq)
    def _():
        send(vs, vown, fs.at[0], fr.at[0], partner)

    @pl.when(z == seq)
    def _():
        copy(vs, vown, fr.at[0])

    wait(vown, fr.at[0])
    wait(voth, fr.at[1])
    mine = vown[...]
    out[0, 0] = lat[0, 0] - 0.8 * (mine + cols[1] * (voth[...].astype(F32) - mine))

    for h in range(HERE):
        wait(heads.at[h, :, 0 : SEQ - 1], xs.at[h])
        for side in range(2):
            wait(rb.at[2 * h + side], bs.at[2 * h + side])
        wait(att.at[h, 0 : ROW - 1], zs.at[h])
        wait(ext.at[h, 8:10], ys.at[h, 0])
        wait(ext.at[h, 2:4], ys.at[h, 1])
    wait(pks.at[0 : ROW - 1], ps)
    wait(pk.at[8:10], pys.at[0])
    wait(pk.at[2:4], pys.at[1])
    wait(sp.at[0 : SEQ - 1], rs)
    wait(vsb, fs.at[1])

    @pl.when(z != seq)
    def _():
        wait(vs, fs.at[0])


def local(
    queries, keys, values, fwd_index, fwd_weight, own_map, back_index, back_weight,
    head_gain, head_shift, head_weight, latents, eye_mix,
):
    hbm = pl.BlockSpec(memory_space=pltpu.HBM)
    vmem = pl.BlockSpec(memory_space=pltpu.VMEM)
    dma = pltpu.SemaphoreType.DMA
    block = (TOK, DH)
    return pl.pallas_call(
        kernel,
        out_shape=jax.ShapeDtypeStruct((1, 1, LAT, TOK), F32),
        in_specs=[hbm] * 13,
        out_specs=vmem,
        scratch_shapes=[
            pltpu.VMEM(fwd_index.shape, jnp.int32),
            pltpu.VMEM(fwd_weight.shape, F32),
            pltpu.VMEM(own_map.shape, jnp.int32),
            pltpu.VMEM(back_index.shape, jnp.int32),
            pltpu.VMEM(back_weight.shape, F32),
            pltpu.VMEM((1, SEQ * FEAT), F32),
            pltpu.VMEM((1, SEQ * FEAT), F32),
            pltpu.VMEM((LAT, SEQ * FEAT), BF),
            pltpu.VMEM((1, 1, LAT, TOK), F32),
            pltpu.VMEM((1, LAT), F32),
            pltpu.VMEM((3, TOK, SEQ * FEAT), BF),
            pltpu.VMEM((HERE, 3, SEQ) + block, BF),
            pltpu.VMEM((2 * HERE, 3) + block, BF),
            pltpu.VMEM((HERE, SEQ) + block, BF),
            pltpu.VMEM((HERE, ROW + 4) + block, BF),
            pltpu.VMEM((SEQ, PACK, TOK), F32),
            pltpu.VMEM((ROW + 4, PACK, TOK), F32),
            pltpu.VMEM((DH, SEQ * TOK), BF),
            pltpu.VMEM((ROW + 2, 6 * TOK, TOK), BF),
            pltpu.VMEM((ROW, 5 * TOK, 2 * TOK), BF),
            pltpu.VMEM((ROW, LAT, TOK), F32),
            pltpu.VMEM((ROW, 2 * HERE, TOK), F32),
            pltpu.VMEM((HERE, 2 * LAT, DH), BF),
            pltpu.VMEM((SEQ, LAT, TOK), F32),
            pltpu.VMEM((HERE, LAT, TOK), F32),
            pltpu.VMEM((2, LAT, TOK), F32),
            pltpu.VMEM((ROW, LAT + 16, TOK), BF),
            pltpu.VMEM((SEQ, LAT + 16, TOK), BF),
            pltpu.VMEM((LAT, TOK), F32),
            pltpu.VMEM((LAT, TOK), BF),
            pltpu.VMEM((LAT, TOK), F32),
            pltpu.VMEM((LAT, TOK), BF),
            dma((10,)),
            dma((3,)),
            dma((HERE,)), dma((HERE,)),
            dma((2 * HERE,)), dma((2 * HERE,)),
            dma((HERE,)), dma((HERE, 3)),
            dma((HERE, 2)), dma((HERE, 2)),
            dma(()), dma((3,)),
            dma((2,)), dma((2,)),
            dma(()), dma(()),
            dma((2,)), dma((2,)),
        ],
        compiler_params=pltpu.CompilerParams(
            collective_id=0, has_side_effects=True, vmem_limit_bytes=60 * 2**20
        ),
    )(
        queries, keys, values, fwd_index, fwd_weight, own_map, back_index, back_weight,
        head_gain.reshape(1, -1), head_shift.reshape(1, -1), head_weight.T, latents,
        eye_mix.reshape(1, -1),
    )


def solution(mesh):
    placed = (
        P("view", "eye", "seq", None),
        P("view", "eye", "seq", None),
        P("view", "eye", "seq", None),
        P("view", "eye", None, None),
        P("view", "eye", None, None),
        P("view", "eye", None, None),
        P("view", "eye", None, None),
        P("view", "eye", None, None),
        P(),
        P(),
        P(),
        P("view", "eye", None, "seq"),
        P(),
    )
    return jax.shard_map(
        local, mesh=mesh, in_specs=placed, out_specs=P("view", "eye", None, "seq"), check_vma=False
    )
```

```python
import math

import jax
import jax.numpy as jnp
from jax import lax
from jax.experimental import pallas as pl
from jax.experimental.pallas import tpu as pltpu
from jax.sharding import PartitionSpec as P

DH = 128
TOK = 128
SEQ = 8
ROW = 8
HERE = 4
FEAT = HERE * DH
LAT = 64
PACK = 40
MESH = pl.DeviceIdType.MESH
BF = jnp.bfloat16
F32 = jnp.float32


def dot(a, b, dims):
    return lax.dot_general(a, b, (dims, ((), ())), preferred_element_type=F32)


def split(x):
    upper = x.astype(BF)
    return upper, (x - upper.astype(F32)).astype(BF)


def wait(ref, sem):
    pltpu.make_async_copy(ref, ref, sem).wait()


def spread(index, weight, rows):
    places = lax.broadcasted_iota(jnp.int32, (rows, TOK), 0).astype(F32)
    total = jnp.zeros((rows, TOK), F32)
    for tap in range(4):
        total = total + jnp.where(places == index[tap : tap + 1], weight[tap : tap + 1], 0.0)
    return total


def kernel(
    q, k, v, fi_in, fw_in, om_in, bi_in, bw_in, gain_in, shift_in, hw_in, lat_in, mix_in, out,
    fi, fw, om, bi, bw, gain, shift, hw, lat, mix,
    kvq, heads, att, ext, pks, pk, vt, jt, mt, acc, stats, wg, gsum, hsum, cols, sp, rp, vs, vsb, vown, voth,
    ins, ks, xs, xr, zs, zr, ys, yr, ps, pr, pys, pyr, rs, rr, fs, fr,
):
    view, eye, seq = lax.axis_index("view"), lax.axis_index("eye"), lax.axis_index("seq")
    row, z = view // ROW, view % ROW
    first = row * ROW
    edge = (z + 2) // 4
    nxt, prv = (view + ROW) % 32, (view + 32 - ROW) % 32
    partner = {"view": first + seq, "eye": eye, "seq": z}
    across = {"view": first + seq, "eye": 1 - eye, "seq": z}

    def along_seq(i):
        return {"view": view, "eye": eye, "seq": i}

    def along_view(i):
        return {"view": i, "eye": eye, "seq": seq}

    def send(src, dst, s, r, target):
        pltpu.make_async_remote_copy(
            src_ref=src, dst_ref=dst, send_sem=s, recv_sem=r, device_id=target, device_id_type=MESH
        ).start()

    def copy(src, dst, s):
        pltpu.make_async_copy(src, dst, s).start()

    small = (
        (fi_in, fi), (fw_in, fw), (om_in, om), (bi_in, bi), (bw_in, bw),
        (gain_in, gain), (shift_in, shift), (hw_in, hw), (lat_in, lat), (mix_in, mix),
    )
    for t, src in enumerate((k, v, q)):
        copy(src.at[0, 0], kvq.at[t], ks.at[t])
    for i, (src, dst) in enumerate(small):
        copy(src, dst, ins.at[i])

    barrier = pltpu.get_barrier_semaphore()

    def greet(target):
        pl.semaphore_signal(barrier, inc=1, device_id=target, device_id_type=MESH)

    for step in range(1, SEQ):
        greet(along_seq((seq + step) % SEQ))
        greet(along_view(first + (z + step) % ROW))
    greet(along_view(nxt))
    greet(along_view(prv))
    greet(across)

    @pl.when(z != seq)
    def _():
        greet(partner)

    pl.semaphore_wait(barrier, 2 * (SEQ - 1) + 3 + jnp.where(z == seq, 0, 1))

    chip, core = seq // 2, seq % 2

    def send_head(h):
        for side in range(2):
            for step in (1, 3, 2, 0):
                other = (chip + step) % 4 * 2 + side
                start = pl.multiple_of((other * HERE + h) * DH, DH)
                block = kvq.at[:, :, pl.ds(start, DH)]
                if step > 0:
                    send(block, heads.at[h, :, seq], xs.at[h], xr.at[h], along_seq(other))
                    continue

                @pl.when(core != side)
                def _():
                    send(block, heads.at[h, :, seq], xs.at[h], xr.at[h], along_seq(other))

                @pl.when(core == side)
                def _():
                    copy(block, heads.at[h, :, seq], xr.at[h])

    for t in range(3):
        wait(kvq.at[t], ks.at[t])
    send_head(0)
    send_head(1)

    for i, (src, dst) in enumerate(small):
        pltpu.make_async_copy(src, dst, ins.at[i]).wait()

    fwd_raw, back_raw = fw[0, 0], bw[0, 0]
    fwd_norm = fwd_raw / jnp.sum(fwd_raw, axis=0, keepdims=True)
    back_norm = back_raw / jnp.sum(back_raw, axis=0, keepdims=True)
    fwd_place, back_place = fi[0, 0].astype(F32), bi[0, 0].astype(F32)
    present = om[0, 0].astype(F32)
    for g in range(SEQ):
        for tile in range(3):
            at = (g * 3 + tile) * TOK
            pks[g, tile * 4 : tile * 4 + 4, :] = fwd_place[:, at : at + TOK]
            pks[g, 12 + tile * 4 : 16 + tile * 4, :] = fwd_norm[:, at : at + TOK]
        at = g * TOK
        pks[g, 24:28, :] = back_place[:, at : at + TOK]
        pks[g, 28:32, :] = back_norm[:, at : at + TOK]
        pks[g, 32:34, :] = present[:, at : at + TOK]
        pks[g, 34:40, :] = jnp.zeros((6, TOK), F32)
    copy(pks.at[z], pk.at[2 + z], pr.at[edge])

    def send_pack(step, _):
        other = (z + step) % ROW
        send(pks.at[other], pk.at[2 + z], ps, pr.at[edge], along_view(first + other))
        return 0

    lax.fori_loop(1, ROW, send_pack, 0)

    send_head(2)
    send_head(3)

    def head_sums(c, carry):
        at = pl.multiple_of(c * FEAT, FEAT)
        turned = hw[:, pl.ds(at, FEAT)].astype(F32)
        gained = jnp.sum(turned * gain[:, pl.ds(at, FEAT)], axis=1, keepdims=True)
        gsum[c] = jnp.broadcast_to(gained, (LAT, TOK))
        return carry + jnp.sum(turned * shift[:, pl.ds(at, FEAT)], axis=1, keepdims=True)

    shift_sum = lax.fori_loop(0, SEQ, head_sums, jnp.zeros((LAT, 1), F32))
    for h in range(HERE):
        at = pl.multiple_of((seq * HERE + h) * DH, DH)
        scaled = hw[:, pl.ds(at, DH)].astype(F32) * gain[:, pl.ds(at, DH)]
        wg[h] = jnp.concatenate(split(scaled), axis=0)
        hsum[h] = jnp.broadcast_to(jnp.sum(scaled, axis=1, keepdims=True), (LAT, TOK))
    diagonal = lax.broadcasted_iota(jnp.int32, (LAT, LAT), 0) == lax.broadcasted_iota(
        jnp.int32, (LAT, LAT), 1
    )
    mix_col = jnp.sum(
        jnp.where(diagonal, jnp.broadcast_to(mix[...], (LAT, LAT)), 0.0), axis=1, keepdims=True
    )
    cols[0] = jnp.broadcast_to(shift_sum, (LAT, TOK))
    cols[1] = jnp.broadcast_to(mix_col, (LAT, TOK))

    rate = math.log2(math.e) / math.sqrt(DH)

    def attend(h):
        wait(heads.at[h], xr.at[h])
        vt[...] = heads[h, 1].reshape(SEQ * TOK, DH).T

        def query_blocks(step, _):
            groups = [(z + 1 + 4 * step + i) % SEQ for i in range(4)]
            keyed = heads[h, 0].reshape(SEQ * TOK, DH)
            rows = [jnp.concatenate([heads[h, 2, g] for g in groups[i : i + 2]], axis=0) for i in (0, 2)]
            scores = [dot(keyed, r, ((1,), (1,))) for r in rows]
            highest = [jnp.max(x, axis=0, keepdims=True) for x in scores]
            probs = [jnp.exp2((x - m) * rate) for x, m in zip(scores, highest)]
            total = [jnp.sum(p, axis=0, keepdims=True) for p in probs]
            mixed = [dot(vt[...], p.astype(BF), ((1,), (0,))) for p in probs]
            mixed = [(m / t).astype(BF) for m, t in zip(mixed, total)]
            for i, g in enumerate(groups):
                att[h, g] = mixed[i // 2][:, i % 2 * TOK : (i % 2 + 1) * TOK]
            for g in groups[:3]:
                send(att.at[h, g], ext.at[h, 2 + z], zs.at[h], zr.at[h, edge], along_view(first + g))
            g = groups[3]

            @pl.when(step == 0)
            def _():
                send(att.at[h, g], ext.at[h, 2 + z], zs.at[h], zr.at[h, edge], along_view(first + g))

            @pl.when(step == 1)
            def _():
                copy(att.at[h, g], ext.at[h, 2 + z], zr.at[h, edge])

            return 0

        lax.fori_loop(0, 2, query_blocks, 0)

    def join(u):
        a0, a1 = pk[u + 1, 32:33, :], pk[u + 1, 33:34, :]
        share = 1.0 / (1.0 + a0 + a1)
        for i, factor in enumerate((a0 * share, share, a1 * share)):
            tile = 2 - i
            part = spread(
                pk[u + i, tile * 4 : tile * 4 + 4, :],
                pk[u + i, 12 + tile * 4 : 16 + tile * 4, :] * factor,
                TOK,
            )
            upper, lower = split(part)
            jt[u, i * TOK : (i + 1) * TOK, :] = upper
            jt[u, (3 + i) * TOK : (4 + i) * TOK, :] = lower


    def compose(w):
        back = spread(pk[w + 2, 24:28, :], pk[w + 2, 28:32, :], 3 * TOK)
        parts = [jnp.zeros((TOK, TOK), F32) for _ in range(5)]
        for b in range(3):
            upper, lower = split(back[b * TOK : (b + 1) * TOK])
            wide = dot(jt[w + b], jnp.concatenate([upper, lower], axis=1), ((1,), (0,)))
            wide = wide[:, :TOK] + wide[:, TOK:]
            wide = wide[: 3 * TOK] + wide[3 * TOK :]
            for i in range(3):
                parts[b + i] = parts[b + i] + wide[i * TOK : (i + 1) * TOK]
        for i in range(5):
            upper, lower = split(parts[i])
            mt[w, i * TOK : (i + 1) * TOK, :TOK] = upper
            mt[w, i * TOK : (i + 1) * TOK, TOK:] = lower

    def in_pairs(count, step):
        def two(i, _):
            step(2 * i)
            step(2 * i + 1)
            return 0

        lax.fori_loop(0, count // 2, two, 0)

    def blend(h, views):
        wide = [
            dot(jnp.concatenate([ext[h, w + i] for i in range(5)], axis=1), mt[w], ((1,), (0,)))
            for w in views
        ]
        x = [a[:, :TOK] + a[:, TOK:] for a in wide]
        mean = [jnp.sum(a, axis=0, keepdims=True) * (1.0 / DH) for a in x]
        centred = [a - m for a, m in zip(x, mean)]
        squares = [jnp.sum(a * a, axis=0, keepdims=True) for a in centred]
        wide = dot(wg[h], jnp.concatenate([a.astype(BF) for a in centred], axis=1), ((1,), (0,)))
        wide = wide[:LAT] + wide[LAT:]
        part = [wide[:, i * TOK : (i + 1) * TOK] for i in range(len(views))]
        if h > 0:
            part = [a + acc[w] for a, w in zip(part, views)]
        for a, m, w in zip(squares, mean, views):
            stats[w, h : h + 1, :] = m
            stats[w, HERE + h : HERE + h + 1, :] = a
        if h < HERE - 1:
            for a, w in zip(part, views):
                acc[w] = a
            return

        for part_here, w in zip(part, views):
            means = stats[w, 0:HERE, :]
            middle = jnp.sum(means, axis=0, keepdims=True) * (1.0 / HERE)
            apart = means - middle
            summed = jnp.sum(stats[w, HERE:, :] + DH * apart * apart, axis=0, keepdims=True)
            for i in range(HERE):
                part_here = part_here + hsum[i] * apart[i : i + 1]
            rows = []
            for line in (middle, summed):
                for _ in range(3):
                    piece = line.astype(BF).astype(F32)
                    rows.append(piece)
                    line = line - piece
            rows.append(jnp.zeros((10, TOK), F32))
            sp[w, 0:LAT, :] = part_here.astype(BF)
            sp[w, LAT:, :] = jnp.concatenate(rows, axis=0).astype(BF)
        for w in views:

            @pl.when(w != seq)
            def _():
                send(sp.at[w], rp.at[seq], rs, rr, along_seq(w))

            @pl.when(w == seq)
            def _():
                copy(sp.at[w], rp.at[seq], rr)

    def forward(h):
        wait(ext.at[h, 2:4], zr.at[h, 0])
        wait(ext.at[h, 8:10], zr.at[h, 2])
        send(ext.at[h, 8:10], ext.at[h, 0:2], ys.at[h, 0], yr.at[h, 0], along_view(nxt))
        send(ext.at[h, 2:4], ext.at[h, 10:12], ys.at[h, 1], yr.at[h, 1], along_view(prv))

    def finish(h):
        wait(ext.at[h, 4:8], zr.at[h, 1])
        blend(h, (2, 3, 4, 5))
        wait(ext.at[h, 0:2], yr.at[h, 0])
        wait(ext.at[h, 10:12], yr.at[h, 1])
        blend(h, (0, 1, 6, 7))

    attend(0)

    wait(pk.at[2:4], pr.at[0])
    wait(pk.at[8:10], pr.at[2])
    send(pk.at[8:10], pk.at[0:2], pys.at[0], pyr.at[0], along_view(nxt))
    send(pk.at[2:4], pk.at[10:12], pys.at[1], pyr.at[1], along_view(prv))

    attend(1)
    wait(pk.at[4:8], pr.at[1])
    wait(pk.at[0:2], pyr.at[0])
    wait(pk.at[10:12], pyr.at[1])
    in_pairs(ROW + 2, join)
    attend(2)
    in_pairs(ROW, compose)
    forward(0)
    finish(0)
    forward(1)
    attend(3)
    forward(2)
    finish(1)
    finish(2)
    forward(3)
    finish(3)
    wait(rp, rr)
    pieces = rp[:, LAT:, :].astype(F32)
    means = pieces[:, 0] + pieces[:, 1] + pieces[:, 2]
    squares = pieces[:, 3] + pieces[:, 4] + pieces[:, 5]
    mean = jnp.sum(means, axis=0, keepdims=True) * (1.0 / SEQ)
    apart = means - mean
    squares = jnp.sum(squares + FEAT * apart * apart, axis=0, keepdims=True)
    deviation = jnp.sqrt(squares * (1.0 / (SEQ * FEAT)) + 1e-06)
    summed = jnp.zeros((LAT, TOK), F32)
    for i in range(SEQ):
        summed = summed + (rp[i, :LAT, :].astype(F32) + gsum[i] * apart[i : i + 1])
    velocity = summed / deviation + cols[0]
    vs[...] = velocity
    vsb[...] = velocity.astype(BF)
    send(vsb, voth, fs.at[1], fr.at[1], across)

    @pl.when(z != seq)
    def _():
        send(vs, vown, fs.at[0], fr.at[0], partner)

    @pl.when(z == seq)
    def _():
        copy(vs, vown, fr.at[0])

    wait(vown, fr.at[0])
    wait(voth, fr.at[1])
    mine = vown[...]
    out[0, 0] = lat[0, 0] - 0.8 * (mine + cols[1] * (voth[...].astype(F32) - mine))

    for h in range(HERE):
        wait(heads.at[h, :, 0 : SEQ - 1], xs.at[h])
        wait(att.at[h, 0 : ROW - 1], zs.at[h])
        wait(ext.at[h, 8:10], ys.at[h, 0])
        wait(ext.at[h, 2:4], ys.at[h, 1])
    wait(pks.at[0 : ROW - 1], ps)
    wait(pk.at[8:10], pys.at[0])
    wait(pk.at[2:4], pys.at[1])
    wait(sp.at[0 : SEQ - 1], rs)
    wait(vsb, fs.at[1])

    @pl.when(z != seq)
    def _():
        wait(vs, fs.at[0])


def local(
    queries, keys, values, fwd_index, fwd_weight, own_map, back_index, back_weight,
    head_gain, head_shift, head_weight, latents, eye_mix,
):
    hbm = pl.BlockSpec(memory_space=pltpu.HBM)
    vmem = pl.BlockSpec(memory_space=pltpu.VMEM)
    dma = pltpu.SemaphoreType.DMA
    block = (TOK, DH)
    return pl.pallas_call(
        kernel,
        out_shape=jax.ShapeDtypeStruct((1, 1, LAT, TOK), F32),
        in_specs=[hbm] * 13,
        out_specs=vmem,
        scratch_shapes=[
            pltpu.VMEM(fwd_index.shape, jnp.int32),
            pltpu.VMEM(fwd_weight.shape, F32),
            pltpu.VMEM(own_map.shape, jnp.int32),
            pltpu.VMEM(back_index.shape, jnp.int32),
            pltpu.VMEM(back_weight.shape, F32),
            pltpu.VMEM((1, SEQ * FEAT), F32),
            pltpu.VMEM((1, SEQ * FEAT), F32),
            pltpu.VMEM((LAT, SEQ * FEAT), BF),
            pltpu.VMEM((1, 1, LAT, TOK), F32),
            pltpu.VMEM((1, LAT), F32),
            pltpu.VMEM((3, TOK, SEQ * FEAT), BF),
            pltpu.VMEM((HERE, 3, SEQ) + block, BF),
            pltpu.VMEM((HERE, SEQ) + block, BF),
            pltpu.VMEM((HERE, ROW + 4) + block, BF),
            pltpu.VMEM((SEQ, PACK, TOK), F32),
            pltpu.VMEM((ROW + 4, PACK, TOK), F32),
            pltpu.VMEM((DH, SEQ * TOK), BF),
            pltpu.VMEM((ROW + 2, 6 * TOK, TOK), BF),
            pltpu.VMEM((ROW, 5 * TOK, 2 * TOK), BF),
            pltpu.VMEM((ROW, LAT, TOK), F32),
            pltpu.VMEM((ROW, 2 * HERE, TOK), F32),
            pltpu.VMEM((HERE, 2 * LAT, DH), BF),
            pltpu.VMEM((SEQ, LAT, TOK), F32),
            pltpu.VMEM((HERE, LAT, TOK), F32),
            pltpu.VMEM((2, LAT, TOK), F32),
            pltpu.VMEM((ROW, LAT + 16, TOK), BF),
            pltpu.VMEM((SEQ, LAT + 16, TOK), BF),
            pltpu.VMEM((LAT, TOK), F32),
            pltpu.VMEM((LAT, TOK), BF),
            pltpu.VMEM((LAT, TOK), F32),
            pltpu.VMEM((LAT, TOK), BF),
            dma((10,)),
            dma((3,)),
            dma((HERE,)), dma((HERE,)),
            dma((HERE,)), dma((HERE, 3)),
            dma((HERE, 2)), dma((HERE, 2)),
            dma(()), dma((3,)),
            dma((2,)), dma((2,)),
            dma(()), dma(()),
            dma((2,)), dma((2,)),
        ],
        compiler_params=pltpu.CompilerParams(
            collective_id=0, has_side_effects=True, vmem_limit_bytes=60 * 2**20
        ),
    )(
        queries, keys, values, fwd_index, fwd_weight, own_map, back_index, back_weight,
        head_gain.reshape(1, -1), head_shift.reshape(1, -1), head_weight.T, latents,
        eye_mix.reshape(1, -1),
    )


def solution(mesh):
    placed = (
        P("view", "eye", "seq", None),
        P("view", "eye", "seq", None),
        P("view", "eye", "seq", None),
        P("view", "eye", None, None),
        P("view", "eye", None, None),
        P("view", "eye", None, None),
        P("view", "eye", None, None),
        P("view", "eye", None, None),
        P(),
        P(),
        P(),
        P("view", "eye", None, "seq"),
        P(),
    )
    return jax.shard_map(
        local, mesh=mesh, in_specs=placed, out_specs=P("view", "eye", None, "seq"), check_vma=False
    )
```

```python
import math

import jax
import jax.numpy as jnp
from jax import lax
from jax.experimental import pallas as pl
from jax.experimental.pallas import tpu as pltpu
from jax.sharding import PartitionSpec as P

DH = 128
TOK = 128
SEQ = 8
ROW = 8
HERE = 4
FEAT = HERE * DH
LAT = 64
PACK = 40
MESH = pl.DeviceIdType.MESH
BF = jnp.bfloat16
F32 = jnp.float32


def dot(a, b, dims):
    return lax.dot_general(a, b, (dims, ((), ())), preferred_element_type=F32)


def split(x):
    upper = x.astype(BF)
    return upper, (x - upper.astype(F32)).astype(BF)


def wait(ref, sem):
    pltpu.make_async_copy(ref, ref, sem).wait()


def spread(index, weight, rows):
    places = lax.broadcasted_iota(jnp.int32, (rows, TOK), 0).astype(F32)
    total = jnp.zeros((rows, TOK), F32)
    for tap in range(4):
        total = total + jnp.where(places == index[tap : tap + 1], weight[tap : tap + 1], 0.0)
    return total


def kernel(
    q, k, v, fi_in, fw_in, om_in, bi_in, bw_in, gain_in, shift_in, hw_in, lat_in, mix_in, out,
    fi, fw, om, bi, bw, gain, shift, hw, lat, mix,
    kvq, heads, rb, att, ext, pks, pk, vt, jt, mt, acc, stats, wg, gsum, hsum, cols, sp, rp, vs, vsb, vown, voth,
    ins, ks, xs, xr, bs, br, zs, zr, ys, yr, ps, pr, pys, pyr, rs, rr, fs, fr,
):
    view, eye, seq = lax.axis_index("view"), lax.axis_index("eye"), lax.axis_index("seq")
    row, z = view // ROW, view % ROW
    first = row * ROW
    edge = (z + 2) // 4
    nxt, prv = (view + ROW) % 32, (view + 32 - ROW) % 32
    partner = {"view": first + seq, "eye": eye, "seq": z}
    across = {"view": first + seq, "eye": 1 - eye, "seq": z}

    def along_seq(i):
        return {"view": view, "eye": eye, "seq": i}

    def along_view(i):
        return {"view": i, "eye": eye, "seq": seq}

    def send(src, dst, s, r, target):
        pltpu.make_async_remote_copy(
            src_ref=src, dst_ref=dst, send_sem=s, recv_sem=r, device_id=target, device_id_type=MESH
        ).start()

    def copy(src, dst, s):
        pltpu.make_async_copy(src, dst, s).start()

    small = (
        (fi_in, fi), (fw_in, fw), (om_in, om), (bi_in, bi), (bw_in, bw),
        (gain_in, gain), (shift_in, shift), (hw_in, hw), (lat_in, lat), (mix_in, mix),
    )
    for t, src in enumerate((k, v, q)):
        copy(src.at[0, 0], kvq.at[t], ks.at[t])
    for i, (src, dst) in enumerate(small):
        copy(src, dst, ins.at[i])

    barrier = pltpu.get_barrier_semaphore()

    def greet(target):
        pl.semaphore_signal(barrier, inc=1, device_id=target, device_id_type=MESH)

    for step in range(1, SEQ):
        greet(along_seq((seq + step) % SEQ))
        greet(along_view(first + (z + step) % ROW))
    greet(along_view(nxt))
    greet(along_view(prv))
    greet(across)

    @pl.when(z != seq)
    def _():
        greet(partner)

    pl.semaphore_wait(barrier, 2 * (SEQ - 1) + 3 + jnp.where(z == seq, 0, 1))

    chip, core = seq // 2, seq % 2
    opposite = (chip + 2) % 4 * 2
    target = (chip + 1 + 2 * core) % 4 * 2
    origin = (chip + 3 - 2 * core) % 4 * 2 + core

    def send_around(h):
        for side in range(2):
            start = pl.multiple_of(((opposite + side) * HERE + h) * DH, DH)
            block = kvq.at[:, :, pl.ds(start, DH)]
            send(block, rb.at[h - 1, side], xs.at[h], br.at[h - 1], along_seq(target + core))

    def hand_on(h):
        wait(rb.at[h - 1], br.at[h - 1])
        for side in range(2):
            send(rb.at[h - 1, side], heads.at[h, :, origin], bs.at[h - 1], xr.at[h], along_seq(target + side))

    def send_head(h):
        for side in range(2):
            for step in (1, 3, 2, 0) if h == 0 else (1, 3, 0):
                other = (chip + step) % 4 * 2 + side
                start = pl.multiple_of((other * HERE + h) * DH, DH)
                block = kvq.at[:, :, pl.ds(start, DH)]
                if step > 0:
                    send(block, heads.at[h, :, seq], xs.at[h], xr.at[h], along_seq(other))
                    continue

                @pl.when(core != side)
                def _():
                    send(block, heads.at[h, :, seq], xs.at[h], xr.at[h], along_seq(other))

                @pl.when(core == side)
                def _():
                    copy(block, heads.at[h, :, seq], xr.at[h])

    for t in range(3):
        wait(kvq.at[t], ks.at[t])
    send_head(0)
    send_around(1)
    send_head(1)
    send_around(2)

    for i, (src, dst) in enumerate(small):
        pltpu.make_async_copy(src, dst, ins.at[i]).wait()

    fwd_raw, back_raw = fw[0, 0], bw[0, 0]
    fwd_norm = fwd_raw / jnp.sum(fwd_raw, axis=0, keepdims=True)
    back_norm = back_raw / jnp.sum(back_raw, axis=0, keepdims=True)
    fwd_place, back_place = fi[0, 0].astype(F32), bi[0, 0].astype(F32)
    present = om[0, 0].astype(F32)
    for g in range(SEQ):
        for tile in range(3):
            at = (g * 3 + tile) * TOK
            pks[g, tile * 4 : tile * 4 + 4, :] = fwd_place[:, at : at + TOK]
            pks[g, 12 + tile * 4 : 16 + tile * 4, :] = fwd_norm[:, at : at + TOK]
        at = g * TOK
        pks[g, 24:28, :] = back_place[:, at : at + TOK]
        pks[g, 28:32, :] = back_norm[:, at : at + TOK]
        pks[g, 32:34, :] = present[:, at : at + TOK]
        pks[g, 34:40, :] = jnp.zeros((6, TOK), F32)
    copy(pks.at[z], pk.at[2 + z], pr.at[edge])

    def send_pack(step, _):
        other = (z + step) % ROW
        send(pks.at[other], pk.at[2 + z], ps, pr.at[edge], along_view(first + other))
        return 0

    lax.fori_loop(1, ROW, send_pack, 0)


    def head_sums(c, carry):
        at = pl.multiple_of(c * FEAT, FEAT)
        turned = hw[:, pl.ds(at, FEAT)].astype(F32)
        gained = jnp.sum(turned * gain[:, pl.ds(at, FEAT)], axis=1, keepdims=True)
        gsum[c] = jnp.broadcast_to(gained, (LAT, TOK))
        return carry + jnp.sum(turned * shift[:, pl.ds(at, FEAT)], axis=1, keepdims=True)

    shift_sum = lax.fori_loop(0, SEQ, head_sums, jnp.zeros((LAT, 1), F32))
    for h in range(HERE):
        at = pl.multiple_of((seq * HERE + h) * DH, DH)
        scaled = hw[:, pl.ds(at, DH)].astype(F32) * gain[:, pl.ds(at, DH)]
        wg[h] = jnp.concatenate(split(scaled), axis=0)
        hsum[h] = jnp.broadcast_to(jnp.sum(scaled, axis=1, keepdims=True), (LAT, TOK))
    diagonal = lax.broadcasted_iota(jnp.int32, (LAT, LAT), 0) == lax.broadcasted_iota(
        jnp.int32, (LAT, LAT), 1
    )
    mix_col = jnp.sum(
        jnp.where(diagonal, jnp.broadcast_to(mix[...], (LAT, LAT)), 0.0), axis=1, keepdims=True
    )
    cols[0] = jnp.broadcast_to(shift_sum, (LAT, TOK))
    cols[1] = jnp.broadcast_to(mix_col, (LAT, TOK))

    rate = math.log2(math.e) / math.sqrt(DH)

    def attend(h):
        wait(heads.at[h], xr.at[h])
        vt[...] = heads[h, 1].reshape(SEQ * TOK, DH).T

        def query_blocks(step, _):
            groups = [(z + 1 + 4 * step + i) % SEQ for i in range(4)]
            keyed = heads[h, 0].reshape(SEQ * TOK, DH)
            rows = [jnp.concatenate([heads[h, 2, g] for g in groups[i : i + 2]], axis=0) for i in (0, 2)]
            scores = [dot(keyed, r, ((1,), (1,))) for r in rows]
            highest = [jnp.max(x, axis=0, keepdims=True) for x in scores]
            probs = [jnp.exp2((x - m) * rate) for x, m in zip(scores, highest)]
            total = [jnp.sum(p, axis=0, keepdims=True) for p in probs]
            mixed = [dot(vt[...], p.astype(BF), ((1,), (0,))) for p in probs]
            mixed = [(m / t).astype(BF) for m, t in zip(mixed, total)]
            for i, g in enumerate(groups):
                att[h, g] = mixed[i // 2][:, i % 2 * TOK : (i % 2 + 1) * TOK]
            for g in groups[:3]:
                send(att.at[h, g], ext.at[h, 2 + z], zs.at[h], zr.at[h, edge], along_view(first + g))
            g = groups[3]

            @pl.when(step == 0)
            def _():
                send(att.at[h, g], ext.at[h, 2 + z], zs.at[h], zr.at[h, edge], along_view(first + g))

            @pl.when(step == 1)
            def _():
                copy(att.at[h, g], ext.at[h, 2 + z], zr.at[h, edge])

            return 0

        lax.fori_loop(0, 2, query_blocks, 0)

    def join(u):
        a0, a1 = pk[u + 1, 32:33, :], pk[u + 1, 33:34, :]
        share = 1.0 / (1.0 + a0 + a1)
        for i, factor in enumerate((a0 * share, share, a1 * share)):
            tile = 2 - i
            part = spread(
                pk[u + i, tile * 4 : tile * 4 + 4, :],
                pk[u + i, 12 + tile * 4 : 16 + tile * 4, :] * factor,
                TOK,
            )
            upper, lower = split(part)
            jt[u, i * TOK : (i + 1) * TOK, :] = upper
            jt[u, (3 + i) * TOK : (4 + i) * TOK, :] = lower


    def compose(w):
        back = spread(pk[w + 2, 24:28, :], pk[w + 2, 28:32, :], 3 * TOK)
        parts = [jnp.zeros((TOK, TOK), F32) for _ in range(5)]
        for b in range(3):
            upper, lower = split(back[b * TOK : (b + 1) * TOK])
            wide = dot(jt[w + b], jnp.concatenate([upper, lower], axis=1), ((1,), (0,)))
            wide = wide[:, :TOK] + wide[:, TOK:]
            wide = wide[: 3 * TOK] + wide[3 * TOK :]
            for i in range(3):
                parts[b + i] = parts[b + i] + wide[i * TOK : (i + 1) * TOK]
        for i in range(5):
            upper, lower = split(parts[i])
            mt[w, i * TOK : (i + 1) * TOK, :TOK] = upper
            mt[w, i * TOK : (i + 1) * TOK, TOK:] = lower

    def in_pairs(count, step):
        def two(i, _):
            step(2 * i)
            step(2 * i + 1)
            return 0

        lax.fori_loop(0, count // 2, two, 0)

    def blend(h, views):
        wide = [
            dot(jnp.concatenate([ext[h, w + i] for i in range(5)], axis=1), mt[w], ((1,), (0,)))
            for w in views
        ]
        x = [a[:, :TOK] + a[:, TOK:] for a in wide]
        mean = [jnp.sum(a, axis=0, keepdims=True) * (1.0 / DH) for a in x]
        centred = [a - m for a, m in zip(x, mean)]
        squares = [jnp.sum(a * a, axis=0, keepdims=True) for a in centred]
        wide = dot(wg[h], jnp.concatenate([a.astype(BF) for a in centred], axis=1), ((1,), (0,)))
        wide = wide[:LAT] + wide[LAT:]
        part = [wide[:, i * TOK : (i + 1) * TOK] for i in range(len(views))]
        if h > 0:
            part = [a + acc[w] for a, w in zip(part, views)]
        for a, m, w in zip(squares, mean, views):
            stats[w, h : h + 1, :] = m
            stats[w, HERE + h : HERE + h + 1, :] = a
        if h < HERE - 1:
            for a, w in zip(part, views):
                acc[w] = a
            return

        for part_here, w in zip(part, views):
            means = stats[w, 0:HERE, :]
            middle = jnp.sum(means, axis=0, keepdims=True) * (1.0 / HERE)
            apart = means - middle
            summed = jnp.sum(stats[w, HERE:, :] + DH * apart * apart, axis=0, keepdims=True)
            for i in range(HERE):
                part_here = part_here + hsum[i] * apart[i : i + 1]
            rows = []
            for line in (middle, summed):
                for _ in range(3):
                    piece = line.astype(BF).astype(F32)
                    rows.append(piece)
                    line = line - piece
            rows.append(jnp.zeros((10, TOK), F32))
            sp[w, 0:LAT, :] = part_here.astype(BF)
            sp[w, LAT:, :] = jnp.concatenate(rows, axis=0).astype(BF)
        for w in views:

            @pl.when(w != seq)
            def _():
                send(sp.at[w], rp.at[seq], rs, rr, along_seq(w))

            @pl.when(w == seq)
            def _():
                copy(sp.at[w], rp.at[seq], rr)

    def forward(h):
        wait(ext.at[h, 2:4], zr.at[h, 0])
        wait(ext.at[h, 8:10], zr.at[h, 2])
        send(ext.at[h, 8:10], ext.at[h, 0:2], ys.at[h, 0], yr.at[h, 0], along_view(nxt))
        send(ext.at[h, 2:4], ext.at[h, 10:12], ys.at[h, 1], yr.at[h, 1], along_view(prv))

    def finish(h):
        wait(ext.at[h, 4:8], zr.at[h, 1])
        blend(h, (2, 3, 4, 5))
        wait(ext.at[h, 0:2], yr.at[h, 0])
        wait(ext.at[h, 10:12], yr.at[h, 1])
        blend(h, (0, 1, 6, 7))

    attend(0)
    hand_on(1)
    send_head(2)
    send_around(3)

    wait(pk.at[2:4], pr.at[0])
    wait(pk.at[8:10], pr.at[2])
    send(pk.at[8:10], pk.at[0:2], pys.at[0], pyr.at[0], along_view(nxt))
    send(pk.at[2:4], pk.at[10:12], pys.at[1], pyr.at[1], along_view(prv))

    attend(1)
    hand_on(2)
    send_head(3)
    wait(pk.at[4:8], pr.at[1])
    wait(pk.at[0:2], pyr.at[0])
    wait(pk.at[10:12], pyr.at[1])
    in_pairs(ROW + 2, join)
    hand_on(3)
    attend(2)
    forward(0)
    forward(1)
    attend(3)
    in_pairs(ROW, compose)
    finish(0)
    forward(2)
    finish(1)
    finish(2)
    forward(3)
    finish(3)
    wait(rp, rr)
    pieces = rp[:, LAT:, :].astype(F32)
    means = pieces[:, 0] + pieces[:, 1] + pieces[:, 2]
    squares = pieces[:, 3] + pieces[:, 4] + pieces[:, 5]
    mean = jnp.sum(means, axis=0, keepdims=True) * (1.0 / SEQ)
    apart = means - mean
    squares = jnp.sum(squares + FEAT * apart * apart, axis=0, keepdims=True)
    deviation = jnp.sqrt(squares * (1.0 / (SEQ * FEAT)) + 1e-06)
    summed = jnp.zeros((LAT, TOK), F32)
    for i in range(SEQ):
        summed = summed + (rp[i, :LAT, :].astype(F32) + gsum[i] * apart[i : i + 1])
    velocity = summed / deviation + cols[0]
    vs[...] = velocity
    vsb[...] = velocity.astype(BF)
    send(vsb, voth, fs.at[1], fr.at[1], across)

    @pl.when(z != seq)
    def _():
        send(vs, vown, fs.at[0], fr.at[0], partner)

    @pl.when(z == seq)
    def _():
        copy(vs, vown, fr.at[0])

    wait(vown, fr.at[0])
    wait(voth, fr.at[1])
    mine = vown[...]
    out[0, 0] = lat[0, 0] - 0.8 * (mine + cols[1] * (voth[...].astype(F32) - mine))

    for h in range(HERE):
        wait(heads.at[h, :, 0 : SEQ - 1], xs.at[h])
        if h > 0:
            wait(rb.at[h - 1], bs.at[h - 1])
        wait(att.at[h, 0 : ROW - 1], zs.at[h])
        wait(ext.at[h, 8:10], ys.at[h, 0])
        wait(ext.at[h, 2:4], ys.at[h, 1])
    wait(pks.at[0 : ROW - 1], ps)
    wait(pk.at[8:10], pys.at[0])
    wait(pk.at[2:4], pys.at[1])
    wait(sp.at[0 : SEQ - 1], rs)
    wait(vsb, fs.at[1])

    @pl.when(z != seq)
    def _():
        wait(vs, fs.at[0])


def local(
    queries, keys, values, fwd_index, fwd_weight, own_map, back_index, back_weight,
    head_gain, head_shift, head_weight, latents, eye_mix,
):
    hbm = pl.BlockSpec(memory_space=pltpu.HBM)
    vmem = pl.BlockSpec(memory_space=pltpu.VMEM)
    dma = pltpu.SemaphoreType.DMA
    block = (TOK, DH)
    return pl.pallas_call(
        kernel,
        out_shape=jax.ShapeDtypeStruct((1, 1, LAT, TOK), F32),
        in_specs=[hbm] * 13,
        out_specs=vmem,
        scratch_shapes=[
            pltpu.VMEM(fwd_index.shape, jnp.int32),
            pltpu.VMEM(fwd_weight.shape, F32),
            pltpu.VMEM(own_map.shape, jnp.int32),
            pltpu.VMEM(back_index.shape, jnp.int32),
            pltpu.VMEM(back_weight.shape, F32),
            pltpu.VMEM((1, SEQ * FEAT), F32),
            pltpu.VMEM((1, SEQ * FEAT), F32),
            pltpu.VMEM((LAT, SEQ * FEAT), BF),
            pltpu.VMEM((1, 1, LAT, TOK), F32),
            pltpu.VMEM((1, LAT), F32),
            pltpu.VMEM((3, TOK, SEQ * FEAT), BF),
            pltpu.VMEM((HERE, 3, SEQ) + block, BF),
            pltpu.VMEM((HERE - 1, 2, 3) + block, BF),
            pltpu.VMEM((HERE, SEQ) + block, BF),
            pltpu.VMEM((HERE, ROW + 4) + block, BF),
            pltpu.VMEM((SEQ, PACK, TOK), F32),
            pltpu.VMEM((ROW + 4, PACK, TOK), F32),
            pltpu.VMEM((DH, SEQ * TOK), BF),
            pltpu.VMEM((ROW + 2, 6 * TOK, TOK), BF),
            pltpu.VMEM((ROW, 5 * TOK, 2 * TOK), BF),
            pltpu.VMEM((ROW, LAT, TOK), F32),
            pltpu.VMEM((ROW, 2 * HERE, TOK), F32),
            pltpu.VMEM((HERE, 2 * LAT, DH), BF),
            pltpu.VMEM((SEQ, LAT, TOK), F32),
            pltpu.VMEM((HERE, LAT, TOK), F32),
            pltpu.VMEM((2, LAT, TOK), F32),
            pltpu.VMEM((ROW, LAT + 16, TOK), BF),
            pltpu.VMEM((SEQ, LAT + 16, TOK), BF),
            pltpu.VMEM((LAT, TOK), F32),
            pltpu.VMEM((LAT, TOK), BF),
            pltpu.VMEM((LAT, TOK), F32),
            pltpu.VMEM((LAT, TOK), BF),
            dma((10,)),
            dma((3,)),
            dma((HERE,)), dma((HERE,)),
            dma((HERE - 1,)), dma((HERE - 1,)),
            dma((HERE,)), dma((HERE, 3)),
            dma((HERE, 2)), dma((HERE, 2)),
            dma(()), dma((3,)),
            dma((2,)), dma((2,)),
            dma(()), dma(()),
            dma((2,)), dma((2,)),
        ],
        compiler_params=pltpu.CompilerParams(
            collective_id=0, has_side_effects=True, vmem_limit_bytes=60 * 2**20
        ),
    )(
        queries, keys, values, fwd_index, fwd_weight, own_map, back_index, back_weight,
        head_gain.reshape(1, -1), head_shift.reshape(1, -1), head_weight.T, latents,
        eye_mix.reshape(1, -1),
    )


def solution(mesh):
    placed = (
        P("view", "eye", "seq", None),
        P("view", "eye", "seq", None),
        P("view", "eye", "seq", None),
        P("view", "eye", None, None),
        P("view", "eye", None, None),
        P("view", "eye", None, None),
        P("view", "eye", None, None),
        P("view", "eye", None, None),
        P(),
        P(),
        P(),
        P("view", "eye", None, "seq"),
        P(),
    )
    return jax.shard_map(
        local, mesh=mesh, in_specs=placed, out_specs=P("view", "eye", None, "seq"), check_vma=False
    )
```

```python
import math

import jax
import jax.numpy as jnp
from jax import lax
from jax.experimental import pallas as pl
from jax.experimental.pallas import tpu as pltpu
from jax.sharding import PartitionSpec as P

DH = 128
TOK = 128
SEQ = 8
ROW = 8
HERE = 4
FEAT = HERE * DH
LAT = 64
PACK = 40
MESH = pl.DeviceIdType.MESH
BF = jnp.bfloat16
F32 = jnp.float32


def dot(a, b, dims):
    return lax.dot_general(a, b, (dims, ((), ())), preferred_element_type=F32)


def split(x):
    upper = x.astype(BF)
    return upper, (x - upper.astype(F32)).astype(BF)


def wait(ref, sem):
    pltpu.make_async_copy(ref, ref, sem).wait()


def spread(index, weight, rows):
    places = lax.broadcasted_iota(jnp.int32, (rows, TOK), 0).astype(F32)
    total = jnp.zeros((rows, TOK), F32)
    for tap in range(4):
        total = total + jnp.where(places == index[tap : tap + 1], weight[tap : tap + 1], 0.0)
    return total


def kernel(
    q, k, v, fi_in, fw_in, om_in, bi_in, bw_in, gain_in, shift_in, hw_in, lat_in, mix_in, out,
    fi, fw, om, bi, bw, gain, shift, hw, lat, mix,
    kvq, heads, att, ext, pks, pk, vt, jt, mt, acc, stats, wg, gsum, hsum, cols, sp, rp, vsb, vown, voth,
    ins, ks, xs, xr, zs, zr, ys, yr, ps, pr, pys, pyr, rs, rr, fs, fr,
):
    view, eye, seq = lax.axis_index("view"), lax.axis_index("eye"), lax.axis_index("seq")
    row, z = view // ROW, view % ROW
    first = row * ROW
    edge = (z + 2) // 4
    nxt, prv = (view + ROW) % 32, (view + 32 - ROW) % 32
    partner = {"view": first + seq, "eye": eye, "seq": z}
    across = {"view": first + seq, "eye": 1 - eye, "seq": z}

    def along_seq(i):
        return {"view": view, "eye": eye, "seq": i}

    def along_view(i):
        return {"view": i, "eye": eye, "seq": seq}

    def send(src, dst, s, r, target):
        pltpu.make_async_remote_copy(
            src_ref=src, dst_ref=dst, send_sem=s, recv_sem=r, device_id=target, device_id_type=MESH
        ).start()

    def copy(src, dst, s):
        pltpu.make_async_copy(src, dst, s).start()

    small = (
        (fi_in, fi), (fw_in, fw), (om_in, om), (bi_in, bi), (bw_in, bw),
        (gain_in, gain), (shift_in, shift), (hw_in, hw), (lat_in, lat), (mix_in, mix),
    )
    for t, src in enumerate((k, v, q)):
        copy(src.at[0, 0], kvq.at[t], ks.at[t])
    barrier = pltpu.get_barrier_semaphore()

    def greet(target):
        pl.semaphore_signal(barrier, inc=1, device_id=target, device_id_type=MESH)

    for step in range(1, SEQ):
        greet(along_seq((seq + step) % SEQ))
        greet(along_view(first + (z + step) % ROW))
    greet(along_view(nxt))
    greet(along_view(prv))
    greet(across)

    @pl.when(z != seq)
    def _():
        greet(partner)

    for i, (src, dst) in enumerate(small):
        copy(src, dst, ins.at[i])

    pl.semaphore_wait(barrier, 2 * (SEQ - 1) + 3 + jnp.where(z == seq, 0, 1))

    chip, core = seq // 2, seq % 2

    def send_head(h):
        for side in range(2):
            for step in (1, 3, 2, 0):
                other = (chip + step) % 4 * 2 + side
                start = pl.multiple_of((other * HERE + h) * DH, DH)
                block = kvq.at[:, :, pl.ds(start, DH)]
                if step > 0:
                    send(block, heads.at[h, :, seq], xs.at[h], xr.at[h], along_seq(other))
                    continue

                @pl.when(core != side)
                def _():
                    send(block, heads.at[h, :, seq], xs.at[h], xr.at[h], along_seq(other))

                @pl.when(core == side)
                def _():
                    copy(block, heads.at[h, :, seq], xr.at[h])

    for t in range(3):
        wait(kvq.at[t], ks.at[t])
    send_head(0)
    send_head(1)

    for i, (src, dst) in enumerate(small):
        pltpu.make_async_copy(src, dst, ins.at[i]).wait()

    fwd_raw, back_raw = fw[0, 0], bw[0, 0]
    fwd_norm = fwd_raw / jnp.sum(fwd_raw, axis=0, keepdims=True)
    back_norm = back_raw / jnp.sum(back_raw, axis=0, keepdims=True)
    fwd_place, back_place = fi[0, 0].astype(F32), bi[0, 0].astype(F32)
    present = om[0, 0].astype(F32)
    for g in range(SEQ):
        for tile in range(3):
            at = (g * 3 + tile) * TOK
            pks[g, tile * 4 : tile * 4 + 4, :] = fwd_place[:, at : at + TOK]
            pks[g, 12 + tile * 4 : 16 + tile * 4, :] = fwd_norm[:, at : at + TOK]
        at = g * TOK
        pks[g, 24:28, :] = back_place[:, at : at + TOK]
        pks[g, 28:32, :] = back_norm[:, at : at + TOK]
        pks[g, 32:34, :] = present[:, at : at + TOK]
        pks[g, 34:40, :] = jnp.zeros((6, TOK), F32)
    copy(pks.at[z], pk.at[2 + z], pr.at[edge])

    def send_pack(step, _):
        other = (z + step) % ROW
        send(pks.at[other], pk.at[2 + z], ps, pr.at[edge], along_view(first + other))
        return 0

    lax.fori_loop(1, ROW, send_pack, 0)

    send_head(2)
    send_head(3)

    def head_sums(c, carry):
        at = pl.multiple_of(c * FEAT, FEAT)
        turned = hw[:, pl.ds(at, FEAT)].astype(F32)
        gained = jnp.sum(turned * gain[:, pl.ds(at, FEAT)], axis=1, keepdims=True)
        gsum[c] = jnp.broadcast_to(gained, (LAT, TOK))
        return carry + jnp.sum(turned * shift[:, pl.ds(at, FEAT)], axis=1, keepdims=True)

    shift_sum = lax.fori_loop(0, SEQ, head_sums, jnp.zeros((LAT, 1), F32))
    for h in range(HERE):
        at = pl.multiple_of((seq * HERE + h) * DH, DH)
        scaled = hw[:, pl.ds(at, DH)].astype(F32) * gain[:, pl.ds(at, DH)]
        wg[h] = jnp.concatenate(split(scaled), axis=0)
        hsum[h] = jnp.broadcast_to(jnp.sum(scaled, axis=1, keepdims=True), (LAT, TOK))
    diagonal = lax.broadcasted_iota(jnp.int32, (LAT, LAT), 0) == lax.broadcasted_iota(
        jnp.int32, (LAT, LAT), 1
    )
    mix_col = jnp.sum(
        jnp.where(diagonal, jnp.broadcast_to(mix[...], (LAT, LAT)), 0.0), axis=1, keepdims=True
    )
    cols[0] = jnp.broadcast_to(shift_sum, (LAT, TOK))
    cols[1] = jnp.broadcast_to(mix_col, (LAT, TOK))

    rate = math.log2(math.e) / math.sqrt(DH)

    def attend(h):
        wait(heads.at[h], xr.at[h])
        vt[...] = heads[h, 1].reshape(SEQ * TOK, DH).T

        def query_blocks(step, _):
            groups = [(z + 1 + 4 * step + i) % SEQ for i in range(4)]
            keyed = heads[h, 0].reshape(SEQ * TOK, DH)
            rows = [jnp.concatenate([heads[h, 2, g] for g in groups[i : i + 2]], axis=0) for i in (0, 2)]
            scores = [dot(keyed, r, ((1,), (1,))) for r in rows]
            highest = [jnp.max(x, axis=0, keepdims=True) for x in scores]
            probs = [jnp.exp2((x - m) * rate) for x, m in zip(scores, highest)]
            total = [jnp.sum(p, axis=0, keepdims=True) for p in probs]
            mixed = [dot(vt[...], p.astype(BF), ((1,), (0,))) for p in probs]
            mixed = [(m / t).astype(BF) for m, t in zip(mixed, total)]
            for i, g in enumerate(groups):
                att[h, g] = mixed[i // 2][:, i % 2 * TOK : (i % 2 + 1) * TOK]
            for g in groups[:3]:
                send(att.at[h, g], ext.at[h, 2 + z], zs.at[h], zr.at[h, edge], along_view(first + g))
            g = groups[3]

            @pl.when(step == 0)
            def _():
                send(att.at[h, g], ext.at[h, 2 + z], zs.at[h], zr.at[h, edge], along_view(first + g))

            @pl.when(step == 1)
            def _():
                copy(att.at[h, g], ext.at[h, 2 + z], zr.at[h, edge])

            return 0

        lax.fori_loop(0, 2, query_blocks, 0)

    def join(u):
        a0, a1 = pk[u + 1, 32:33, :], pk[u + 1, 33:34, :]
        share = 1.0 / (1.0 + a0 + a1)
        for i, factor in enumerate((a0 * share, share, a1 * share)):
            tile = 2 - i
            part = spread(
                pk[u + i, tile * 4 : tile * 4 + 4, :],
                pk[u + i, 12 + tile * 4 : 16 + tile * 4, :] * factor,
                TOK,
            )
            upper, lower = split(part)
            jt[u, i * TOK : (i + 1) * TOK, :] = upper
            jt[u, (3 + i) * TOK : (4 + i) * TOK, :] = lower


    def compose(w):
        back = spread(pk[w + 2, 24:28, :], pk[w + 2, 28:32, :], 3 * TOK)
        parts = [jnp.zeros((TOK, TOK), F32) for _ in range(5)]
        for b in range(3):
            upper, lower = split(back[b * TOK : (b + 1) * TOK])
            wide = dot(jt[w + b], jnp.concatenate([upper, lower], axis=1), ((1,), (0,)))
            wide = wide[:, :TOK] + wide[:, TOK:]
            wide = wide[: 3 * TOK] + wide[3 * TOK :]
            for i in range(3):
                parts[b + i] = parts[b + i] + wide[i * TOK : (i + 1) * TOK]
        for i in range(5):
            upper, lower = split(parts[i])
            mt[w, i * TOK : (i + 1) * TOK, :TOK] = upper
            mt[w, i * TOK : (i + 1) * TOK, TOK:] = lower

    def in_pairs(count, step):
        def two(i, _):
            step(2 * i)
            step(2 * i + 1)
            return 0

        lax.fori_loop(0, count // 2, two, 0)

    def blend(h, views):
        wide = [
            dot(jnp.concatenate([ext[h, w + i] for i in range(5)], axis=1), mt[w], ((1,), (0,)))
            for w in views
        ]
        x = [a[:, :TOK] + a[:, TOK:] for a in wide]
        mean = [jnp.sum(a, axis=0, keepdims=True) * (1.0 / DH) for a in x]
        centred = [a - m for a, m in zip(x, mean)]
        squares = [jnp.sum(a * a, axis=0, keepdims=True) for a in centred]
        wide = dot(wg[h], jnp.concatenate([a.astype(BF) for a in centred], axis=1), ((1,), (0,)))
        wide = wide[:LAT] + wide[LAT:]
        part = [wide[:, i * TOK : (i + 1) * TOK] for i in range(len(views))]
        if h > 0:
            part = [a + acc[w] for a, w in zip(part, views)]
        for a, m, w in zip(squares, mean, views):
            stats[w, h : h + 1, :] = m
            stats[w, HERE + h : HERE + h + 1, :] = a
        if h < HERE - 1:
            for a, w in zip(part, views):
                acc[w] = a
            return

        for part_here, w in zip(part, views):
            means = stats[w, 0:HERE, :]
            middle = jnp.sum(means, axis=0, keepdims=True) * (1.0 / HERE)
            apart = means - middle
            summed = jnp.sum(stats[w, HERE:, :] + DH * apart * apart, axis=0, keepdims=True)
            for i in range(HERE):
                part_here = part_here + hsum[i] * apart[i : i + 1]
            rows = []
            for line in (middle, summed):
                for _ in range(3):
                    piece = line.astype(BF).astype(F32)
                    rows.append(piece)
                    line = line - piece
            rows.append(jnp.zeros((10, TOK), F32))
            sp[w, 0:LAT, :] = part_here.astype(BF)
            sp[w, LAT:, :] = jnp.concatenate(rows, axis=0).astype(BF)
        for w in views:

            @pl.when(w != seq)
            def _():
                send(sp.at[w], rp.at[seq], rs, rr, along_seq(w))

            @pl.when(w == seq)
            def _():
                copy(sp.at[w], rp.at[seq], rr)

    def forward(h):
        wait(ext.at[h, 8:10], zr.at[h, 2])
        send(ext.at[h, 8:10], ext.at[h, 0:2], ys.at[h, 0], yr.at[h, 0], along_view(nxt))
        wait(ext.at[h, 2:4], zr.at[h, 0])
        send(ext.at[h, 2:4], ext.at[h, 10:12], ys.at[h, 1], yr.at[h, 1], along_view(prv))

    def finish(h):
        wait(ext.at[h, 4:8], zr.at[h, 1])
        blend(h, (2, 3, 4, 5))
        wait(ext.at[h, 0:2], yr.at[h, 0])
        wait(ext.at[h, 10:12], yr.at[h, 1])
        blend(h, (0, 1, 6, 7))

    attend(0)

    wait(pk.at[2:4], pr.at[0])
    wait(pk.at[8:10], pr.at[2])
    send(pk.at[8:10], pk.at[0:2], pys.at[0], pyr.at[0], along_view(nxt))
    send(pk.at[2:4], pk.at[10:12], pys.at[1], pyr.at[1], along_view(prv))

    attend(1)
    wait(pk.at[4:8], pr.at[1])
    wait(pk.at[0:2], pyr.at[0])
    wait(pk.at[10:12], pyr.at[1])
    in_pairs(ROW + 2, join)
    attend(2)
    in_pairs(ROW, compose)
    forward(0)
    finish(0)
    forward(1)
    attend(3)
    forward(2)
    finish(1)
    finish(2)
    forward(3)
    finish(3)
    wait(rp, rr)
    pieces = rp[:, LAT:, :].astype(F32)
    means = pieces[:, 0] + pieces[:, 1] + pieces[:, 2]
    squares = pieces[:, 3] + pieces[:, 4] + pieces[:, 5]
    mean = jnp.sum(means, axis=0, keepdims=True) * (1.0 / SEQ)
    apart = means - mean
    squares = jnp.sum(squares + FEAT * apart * apart, axis=0, keepdims=True)
    deviation = jnp.sqrt(squares * (1.0 / (SEQ * FEAT)) + 1e-06)
    summed = jnp.zeros((LAT, TOK), F32)
    for i in range(SEQ):
        summed = summed + (rp[i, :LAT, :].astype(F32) + gsum[i] * apart[i : i + 1])
    velocity = summed / deviation + cols[0]
    vsb[...] = velocity.astype(BF)
    send(vsb, voth, fs.at[1], fr.at[1], across)

    @pl.when(z != seq)
    def _():
        send(vsb, vown, fs.at[0], fr.at[0], partner)

    @pl.when(z == seq)
    def _():
        copy(vsb, vown, fr.at[0])

    for h in range(HERE):
        wait(heads.at[h, :, 0 : SEQ - 1], xs.at[h])
        wait(att.at[h, 0 : ROW - 1], zs.at[h])
        wait(ext.at[h, 8:10], ys.at[h, 0])
        wait(ext.at[h, 2:4], ys.at[h, 1])
    wait(pks.at[0 : ROW - 1], ps)
    wait(pk.at[8:10], pys.at[0])
    wait(pk.at[2:4], pys.at[1])
    wait(sp.at[0 : SEQ - 1], rs)

    wait(vown, fr.at[0])
    wait(voth, fr.at[1])
    mine = vown[...].astype(F32)
    out[0, 0] = lat[0, 0] - 0.8 * (mine + cols[1] * (voth[...].astype(F32) - mine))

    wait(vsb, fs.at[1])

    @pl.when(z != seq)
    def _():
        wait(vsb, fs.at[0])


def local(
    queries, keys, values, fwd_index, fwd_weight, own_map, back_index, back_weight,
    head_gain, head_shift, head_weight, latents, eye_mix,
):
    hbm = pl.BlockSpec(memory_space=pltpu.HBM)
    vmem = pl.BlockSpec(memory_space=pltpu.VMEM)
    dma = pltpu.SemaphoreType.DMA
    block = (TOK, DH)
    return pl.pallas_call(
        kernel,
        out_shape=jax.ShapeDtypeStruct((1, 1, LAT, TOK), F32),
        in_specs=[hbm] * 13,
        out_specs=vmem,
        scratch_shapes=[
            pltpu.VMEM(fwd_index.shape, jnp.int32),
            pltpu.VMEM(fwd_weight.shape, F32),
            pltpu.VMEM(own_map.shape, jnp.int32),
            pltpu.VMEM(back_index.shape, jnp.int32),
            pltpu.VMEM(back_weight.shape, F32),
            pltpu.VMEM((1, SEQ * FEAT), F32),
            pltpu.VMEM((1, SEQ * FEAT), F32),
            pltpu.VMEM((LAT, SEQ * FEAT), BF),
            pltpu.VMEM((1, 1, LAT, TOK), F32),
            pltpu.VMEM((1, LAT), F32),
            pltpu.VMEM((3, TOK, SEQ * FEAT), BF),
            pltpu.VMEM((HERE, 3, SEQ) + block, BF),
            pltpu.VMEM((HERE, SEQ) + block, BF),
            pltpu.VMEM((HERE, ROW + 4) + block, BF),
            pltpu.VMEM((SEQ, PACK, TOK), F32),
            pltpu.VMEM((ROW + 4, PACK, TOK), F32),
            pltpu.VMEM((DH, SEQ * TOK), BF),
            pltpu.VMEM((ROW + 2, 6 * TOK, TOK), BF),
            pltpu.VMEM((ROW, 5 * TOK, 2 * TOK), BF),
            pltpu.VMEM((ROW, LAT, TOK), F32),
            pltpu.VMEM((ROW, 2 * HERE, TOK), F32),
            pltpu.VMEM((HERE, 2 * LAT, DH), BF),
            pltpu.VMEM((SEQ, LAT, TOK), F32),
            pltpu.VMEM((HERE, LAT, TOK), F32),
            pltpu.VMEM((2, LAT, TOK), F32),
            pltpu.VMEM((ROW, LAT + 16, TOK), BF),
            pltpu.VMEM((SEQ, LAT + 16, TOK), BF),
            pltpu.VMEM((LAT, TOK), BF),
            pltpu.VMEM((LAT, TOK), BF),
            pltpu.VMEM((LAT, TOK), BF),
            dma((10,)),
            dma((3,)),
            dma((HERE,)), dma((HERE,)),
            dma((HERE,)), dma((HERE, 3)),
            dma((HERE, 2)), dma((HERE, 2)),
            dma(()), dma((3,)),
            dma((2,)), dma((2,)),
            dma(()), dma(()),
            dma((2,)), dma((2,)),
        ],
        compiler_params=pltpu.CompilerParams(
            collective_id=0, has_side_effects=True, vmem_limit_bytes=60 * 2**20
        ),
    )(
        queries, keys, values, fwd_index, fwd_weight, own_map, back_index, back_weight,
        head_gain.reshape(1, -1), head_shift.reshape(1, -1), head_weight.T, latents,
        eye_mix.reshape(1, -1),
    )


def solution(mesh):
    placed = (
        P("view", "eye", "seq", None),
        P("view", "eye", "seq", None),
        P("view", "eye", "seq", None),
        P("view", "eye", None, None),
        P("view", "eye", None, None),
        P("view", "eye", None, None),
        P("view", "eye", None, None),
        P("view", "eye", None, None),
        P(),
        P(),
        P(),
        P("view", "eye", None, "seq"),
        P(),
    )
    return jax.shard_map(
        local, mesh=mesh, in_specs=placed, out_specs=P("view", "eye", None, "seq"), check_vma=False
    )
```

```python
import math

import jax
import jax.numpy as jnp
from jax import lax
from jax.experimental import pallas as pl
from jax.experimental.pallas import tpu as pltpu
from jax.sharding import PartitionSpec as P

DH = 128
TOK = 128
SEQ = 8
ROW = 8
HERE = 4
FEAT = HERE * DH
LAT = 64
PACK = 40
MESH = pl.DeviceIdType.MESH
BF = jnp.bfloat16
F32 = jnp.float32


def dot(a, b, dims):
    return lax.dot_general(a, b, (dims, ((), ())), preferred_element_type=F32)


def split(x):
    upper = x.astype(BF)
    return upper, (x - upper.astype(F32)).astype(BF)


def wait(ref, sem):
    pltpu.make_async_copy(ref, ref, sem).wait()


def spread(index, weight, rows):
    places = lax.broadcasted_iota(jnp.int32, (rows, TOK), 0).astype(F32)
    total = jnp.zeros((rows, TOK), F32)
    for tap in range(4):
        total = total + jnp.where(places == index[tap : tap + 1], weight[tap : tap + 1], 0.0)
    return total


def kernel(
    q, k, v, fi_in, fw_in, om_in, bi_in, bw_in, gain_in, shift_in, hw_in, lat_in, mix_in, out,
    fi, fw, om, bi, bw, gain, shift, hw, lat, mix,
    kvq, heads, att, ext, pks, pk, vt, jt, mt, acc, stats, wg, gsum, hsum, cols, sp, rp, vsb, vown, voth,
    ins, ks, xs, xr, xq, zs, zr, ys, yr, ps, pr, pys, pyr, rs, rr, fs, fr,
):
    view, eye, seq = lax.axis_index("view"), lax.axis_index("eye"), lax.axis_index("seq")
    row, z = view // ROW, view % ROW
    first = row * ROW
    edge = (z + 2) // 4
    nxt, prv = (view + ROW) % 32, (view + 32 - ROW) % 32
    partner = {"view": first + seq, "eye": eye, "seq": z}
    across = {"view": first + seq, "eye": 1 - eye, "seq": z}

    def along_seq(i):
        return {"view": view, "eye": eye, "seq": i}

    def along_view(i):
        return {"view": i, "eye": eye, "seq": seq}

    def send(src, dst, s, r, target):
        pltpu.make_async_remote_copy(
            src_ref=src, dst_ref=dst, send_sem=s, recv_sem=r, device_id=target, device_id_type=MESH
        ).start()

    def copy(src, dst, s):
        pltpu.make_async_copy(src, dst, s).start()

    small = (
        (fi_in, fi), (fw_in, fw), (om_in, om), (bi_in, bi), (bw_in, bw),
        (gain_in, gain), (shift_in, shift), (hw_in, hw), (lat_in, lat), (mix_in, mix),
    )
    for t, src in enumerate((k, v, q)):
        copy(src.at[0, 0], kvq.at[t], ks.at[t])
    barrier = pltpu.get_barrier_semaphore()

    def greet(target):
        pl.semaphore_signal(barrier, inc=1, device_id=target, device_id_type=MESH)

    for step in range(1, SEQ):
        greet(along_seq((seq + step) % SEQ))
        greet(along_view(first + (z + step) % ROW))
    greet(along_view(nxt))
    greet(along_view(prv))
    greet(across)

    @pl.when(z != seq)
    def _():
        greet(partner)

    for i, (src, dst) in enumerate(small):
        copy(src, dst, ins.at[i])

    pl.semaphore_wait(barrier, 2 * (SEQ - 1) + 3 + jnp.where(z == seq, 0, 1))

    chip, core = seq // 2, seq % 2

    def send_head(h):
        last = h == HERE - 1
        for side in range(2):
            for begin, count in ((0, 2), (2, 1)) if last else ((0, 3),):
                for step in (1, 3, 2, 0):
                    other = (chip + step) % 4 * 2 + side
                    start = pl.multiple_of((other * HERE + h) * DH, DH)
                    block = kvq.at[begin : begin + count, :, pl.ds(start, DH)]
                    place = heads.at[h, begin : begin + count, seq]
                    sem = xr.at[h] if begin == 0 else xq.at[0 if step in (1, 3) else 1]
                    if step > 0:
                        send(block, place, xs.at[h], sem, along_seq(other))
                        continue

                    @pl.when(core != side)
                    def _():
                        send(block, place, xs.at[h], sem, along_seq(other))

                    @pl.when(core == side)
                    def _():
                        copy(block, place, sem)

    for t in range(3):
        wait(kvq.at[t], ks.at[t])
    send_head(0)
    send_head(1)

    for i, (src, dst) in enumerate(small):
        pltpu.make_async_copy(src, dst, ins.at[i]).wait()

    fwd_raw, back_raw = fw[0, 0], bw[0, 0]
    fwd_norm = fwd_raw / jnp.sum(fwd_raw, axis=0, keepdims=True)
    back_norm = back_raw / jnp.sum(back_raw, axis=0, keepdims=True)
    fwd_place, back_place = fi[0, 0].astype(F32), bi[0, 0].astype(F32)
    present = om[0, 0].astype(F32)
    for g in range(SEQ):
        for tile in range(3):
            at = (g * 3 + tile) * TOK
            pks[g, tile * 4 : tile * 4 + 4, :] = fwd_place[:, at : at + TOK]
            pks[g, 12 + tile * 4 : 16 + tile * 4, :] = fwd_norm[:, at : at + TOK]
        at = g * TOK
        pks[g, 24:28, :] = back_place[:, at : at + TOK]
        pks[g, 28:32, :] = back_norm[:, at : at + TOK]
        pks[g, 32:34, :] = present[:, at : at + TOK]
        pks[g, 34:40, :] = jnp.zeros((6, TOK), F32)
    copy(pks.at[z], pk.at[2 + z], pr.at[edge])

    def send_pack(step, _):
        other = (z + step) % ROW
        send(pks.at[other], pk.at[2 + z], ps, pr.at[edge], along_view(first + other))
        return 0

    lax.fori_loop(1, ROW, send_pack, 0)

    send_head(2)
    send_head(3)

    def head_sums(c, carry):
        at = pl.multiple_of(c * FEAT, FEAT)
        turned = hw[:, pl.ds(at, FEAT)].astype(F32)
        gained = jnp.sum(turned * gain[:, pl.ds(at, FEAT)], axis=1, keepdims=True)
        gsum[c] = jnp.broadcast_to(gained, (LAT, TOK))
        return carry + jnp.sum(turned * shift[:, pl.ds(at, FEAT)], axis=1, keepdims=True)

    shift_sum = lax.fori_loop(0, SEQ, head_sums, jnp.zeros((LAT, 1), F32))
    for h in range(HERE):
        at = pl.multiple_of((seq * HERE + h) * DH, DH)
        scaled = hw[:, pl.ds(at, DH)].astype(F32) * gain[:, pl.ds(at, DH)]
        wg[h] = jnp.concatenate(split(scaled), axis=0)
        hsum[h] = jnp.broadcast_to(jnp.sum(scaled, axis=1, keepdims=True), (LAT, TOK))
    diagonal = lax.broadcasted_iota(jnp.int32, (LAT, LAT), 0) == lax.broadcasted_iota(
        jnp.int32, (LAT, LAT), 1
    )
    mix_col = jnp.sum(
        jnp.where(diagonal, jnp.broadcast_to(mix[...], (LAT, LAT)), 0.0), axis=1, keepdims=True
    )
    cols[0] = jnp.broadcast_to(shift_sum, (LAT, TOK))
    cols[1] = jnp.broadcast_to(mix_col, (LAT, TOK))

    rate = math.log2(math.e) / math.sqrt(DH)

    def query_blocks(h, groups):
        keyed = heads[h, 0].reshape(SEQ * TOK, DH)
        rows = [jnp.concatenate([heads[h, 2, g] for g in groups[i : i + 2]], axis=0) for i in (0, 2)]
        scores = [dot(keyed, r, ((1,), (1,))) for r in rows]
        highest = [jnp.max(x, axis=0, keepdims=True) for x in scores]
        probs = [jnp.exp2((x - m) * rate) for x, m in zip(scores, highest)]
        total = [jnp.sum(p, axis=0, keepdims=True) for p in probs]
        mixed = [dot(vt[...], p.astype(BF), ((1,), (0,))) for p in probs]
        mixed = [(m / t).astype(BF) for m, t in zip(mixed, total)]
        for i, g in enumerate(groups):
            att[h, g] = mixed[i // 2][:, i % 2 * TOK : (i % 2 + 1) * TOK]

    def send_group(h, g):
        send(att.at[h, g], ext.at[h, 2 + z], zs.at[h], zr.at[h, edge], along_view(first + g))

    def keep_group(h, g):
        copy(att.at[h, g], ext.at[h, 2 + z], zr.at[h, edge])

    def attend(h):
        wait(heads.at[h], xr.at[h])
        vt[...] = heads[h, 1].reshape(SEQ * TOK, DH).T

        def one(step, _):
            groups = [(z + 1 + 4 * step + i) % SEQ for i in range(4)]
            query_blocks(h, groups)
            for g in groups[:3]:
                send_group(h, g)
            pl.when(step == 0)(lambda: send_group(h, groups[3]))
            pl.when(step == 1)(lambda: keep_group(h, groups[3]))
            return 0

        lax.fori_loop(0, 2, one, 0)

    def attend_last(h):
        wait(heads.at[h, 0:2], xr.at[h])
        vt[...] = heads[h, 1].reshape(SEQ * TOK, DH).T
        for i, steps in enumerate(((1, 3), (2, 0))):
            wait(heads.at[h, 2, 0:4], xq.at[i])
            groups = [(chip + step) % 4 * 2 + side for step in steps for side in range(2)]
            query_blocks(h, groups)
            for g in groups:
                pl.when(g != z)(lambda g=g: send_group(h, g))
                pl.when(g == z)(lambda g=g: keep_group(h, g))

    def join(u):
        a0, a1 = pk[u + 1, 32:33, :], pk[u + 1, 33:34, :]
        share = 1.0 / (1.0 + a0 + a1)
        for i, factor in enumerate((a0 * share, share, a1 * share)):
            tile = 2 - i
            part = spread(
                pk[u + i, tile * 4 : tile * 4 + 4, :],
                pk[u + i, 12 + tile * 4 : 16 + tile * 4, :] * factor,
                TOK,
            )
            upper, lower = split(part)
            jt[u, i * TOK : (i + 1) * TOK, :] = upper
            jt[u, (3 + i) * TOK : (4 + i) * TOK, :] = lower


    def compose(w):
        back = spread(pk[w + 2, 24:28, :], pk[w + 2, 28:32, :], 3 * TOK)
        parts = [jnp.zeros((TOK, TOK), F32) for _ in range(5)]
        for b in range(3):
            upper, lower = split(back[b * TOK : (b + 1) * TOK])
            wide = dot(jt[w + b], jnp.concatenate([upper, lower], axis=1), ((1,), (0,)))
            wide = wide[:, :TOK] + wide[:, TOK:]
            wide = wide[: 3 * TOK] + wide[3 * TOK :]
            for i in range(3):
                parts[b + i] = parts[b + i] + wide[i * TOK : (i + 1) * TOK]
        for i in range(5):
            upper, lower = split(parts[i])
            mt[w, i * TOK : (i + 1) * TOK, :TOK] = upper
            mt[w, i * TOK : (i + 1) * TOK, TOK:] = lower

    def in_pairs(count, step):
        def two(i, _):
            step(2 * i)
            step(2 * i + 1)
            return 0

        lax.fori_loop(0, count // 2, two, 0)

    def blend(h, views):
        wide = [
            dot(jnp.concatenate([ext[h, w + i] for i in range(5)], axis=1), mt[w], ((1,), (0,)))
            for w in views
        ]
        x = [a[:, :TOK] + a[:, TOK:] for a in wide]
        mean = [jnp.sum(a, axis=0, keepdims=True) * (1.0 / DH) for a in x]
        centred = [a - m for a, m in zip(x, mean)]
        squares = [jnp.sum(a * a, axis=0, keepdims=True) for a in centred]
        wide = dot(wg[h], jnp.concatenate([a.astype(BF) for a in centred], axis=1), ((1,), (0,)))
        wide = wide[:LAT] + wide[LAT:]
        part = [wide[:, i * TOK : (i + 1) * TOK] for i in range(len(views))]
        if h > 0:
            part = [a + acc[w] for a, w in zip(part, views)]
        for a, m, w in zip(squares, mean, views):
            stats[w, h : h + 1, :] = m
            stats[w, HERE + h : HERE + h + 1, :] = a
        if h < HERE - 1:
            for a, w in zip(part, views):
                acc[w] = a
            return

        for part_here, w in zip(part, views):
            means = stats[w, 0:HERE, :]
            middle = jnp.sum(means, axis=0, keepdims=True) * (1.0 / HERE)
            apart = means - middle
            summed = jnp.sum(stats[w, HERE:, :] + DH * apart * apart, axis=0, keepdims=True)
            for i in range(HERE):
                part_here = part_here + hsum[i] * apart[i : i + 1]
            rows = []
            for line in (middle, summed):
                for _ in range(3):
                    piece = line.astype(BF).astype(F32)
                    rows.append(piece)
                    line = line - piece
            rows.append(jnp.zeros((10, TOK), F32))
            sp[w, 0:LAT, :] = part_here.astype(BF)
            sp[w, LAT:, :] = jnp.concatenate(rows, axis=0).astype(BF)
        for w in views:

            @pl.when(w != seq)
            def _():
                send(sp.at[w], rp.at[seq], rs, rr, along_seq(w))

            @pl.when(w == seq)
            def _():
                copy(sp.at[w], rp.at[seq], rr)

    def forward(h):
        wait(ext.at[h, 8:10], zr.at[h, 2])
        send(ext.at[h, 8:10], ext.at[h, 0:2], ys.at[h, 0], yr.at[h, 0], along_view(nxt))
        wait(ext.at[h, 2:4], zr.at[h, 0])
        send(ext.at[h, 2:4], ext.at[h, 10:12], ys.at[h, 1], yr.at[h, 1], along_view(prv))

    def finish(h):
        wait(ext.at[h, 4:8], zr.at[h, 1])
        blend(h, (2, 3, 4, 5))
        wait(ext.at[h, 0:2], yr.at[h, 0])
        wait(ext.at[h, 10:12], yr.at[h, 1])
        blend(h, (0, 1, 6, 7))

    attend(0)

    wait(pk.at[2:4], pr.at[0])
    wait(pk.at[8:10], pr.at[2])
    send(pk.at[8:10], pk.at[0:2], pys.at[0], pyr.at[0], along_view(nxt))
    send(pk.at[2:4], pk.at[10:12], pys.at[1], pyr.at[1], along_view(prv))

    attend(1)
    wait(pk.at[4:8], pr.at[1])
    wait(pk.at[0:2], pyr.at[0])
    wait(pk.at[10:12], pyr.at[1])
    in_pairs(ROW + 2, join)
    attend(2)
    in_pairs(ROW, compose)
    forward(0)
    finish(0)
    forward(1)
    attend_last(3)
    forward(2)
    finish(1)
    finish(2)
    forward(3)
    finish(3)
    wait(rp, rr)
    pieces = rp[:, LAT:, :].astype(F32)
    means = pieces[:, 0] + pieces[:, 1] + pieces[:, 2]
    squares = pieces[:, 3] + pieces[:, 4] + pieces[:, 5]
    mean = jnp.sum(means, axis=0, keepdims=True) * (1.0 / SEQ)
    apart = means - mean
    squares = jnp.sum(squares + FEAT * apart * apart, axis=0, keepdims=True)
    deviation = jnp.sqrt(squares * (1.0 / (SEQ * FEAT)) + 1e-06)
    summed = jnp.zeros((LAT, TOK), F32)
    for i in range(SEQ):
        summed = summed + (rp[i, :LAT, :].astype(F32) + gsum[i] * apart[i : i + 1])
    velocity = summed / deviation + cols[0]
    vsb[...] = velocity.astype(BF)
    send(vsb, voth, fs.at[1], fr.at[1], across)

    @pl.when(z != seq)
    def _():
        send(vsb, vown, fs.at[0], fr.at[0], partner)

    @pl.when(z == seq)
    def _():
        copy(vsb, vown, fr.at[0])

    for h in range(HERE):
        wait(heads.at[h, :, 0 : SEQ - 1], xs.at[h])
        wait(att.at[h, 0 : ROW - 1], zs.at[h])
        wait(ext.at[h, 8:10], ys.at[h, 0])
        wait(ext.at[h, 2:4], ys.at[h, 1])
    wait(pks.at[0 : ROW - 1], ps)
    wait(pk.at[8:10], pys.at[0])
    wait(pk.at[2:4], pys.at[1])
    wait(sp.at[0 : SEQ - 1], rs)

    wait(vown, fr.at[0])
    wait(voth, fr.at[1])
    mine = vown[...].astype(F32)
    out[0, 0] = lat[0, 0] - 0.8 * (mine + cols[1] * (voth[...].astype(F32) - mine))

    wait(vsb, fs.at[1])

    @pl.when(z != seq)
    def _():
        wait(vsb, fs.at[0])


def local(
    queries, keys, values, fwd_index, fwd_weight, own_map, back_index, back_weight,
    head_gain, head_shift, head_weight, latents, eye_mix,
):
    hbm = pl.BlockSpec(memory_space=pltpu.HBM)
    vmem = pl.BlockSpec(memory_space=pltpu.VMEM)
    dma = pltpu.SemaphoreType.DMA
    block = (TOK, DH)
    return pl.pallas_call(
        kernel,
        out_shape=jax.ShapeDtypeStruct((1, 1, LAT, TOK), F32),
        in_specs=[hbm] * 13,
        out_specs=vmem,
        scratch_shapes=[
            pltpu.VMEM(fwd_index.shape, jnp.int32),
            pltpu.VMEM(fwd_weight.shape, F32),
            pltpu.VMEM(own_map.shape, jnp.int32),
            pltpu.VMEM(back_index.shape, jnp.int32),
            pltpu.VMEM(back_weight.shape, F32),
            pltpu.VMEM((1, SEQ * FEAT), F32),
            pltpu.VMEM((1, SEQ * FEAT), F32),
            pltpu.VMEM((LAT, SEQ * FEAT), BF),
            pltpu.VMEM((1, 1, LAT, TOK), F32),
            pltpu.VMEM((1, LAT), F32),
            pltpu.VMEM((3, TOK, SEQ * FEAT), BF),
            pltpu.VMEM((HERE, 3, SEQ) + block, BF),
            pltpu.VMEM((HERE, SEQ) + block, BF),
            pltpu.VMEM((HERE, ROW + 4) + block, BF),
            pltpu.VMEM((SEQ, PACK, TOK), F32),
            pltpu.VMEM((ROW + 4, PACK, TOK), F32),
            pltpu.VMEM((DH, SEQ * TOK), BF),
            pltpu.VMEM((ROW + 2, 6 * TOK, TOK), BF),
            pltpu.VMEM((ROW, 5 * TOK, 2 * TOK), BF),
            pltpu.VMEM((ROW, LAT, TOK), F32),
            pltpu.VMEM((ROW, 2 * HERE, TOK), F32),
            pltpu.VMEM((HERE, 2 * LAT, DH), BF),
            pltpu.VMEM((SEQ, LAT, TOK), F32),
            pltpu.VMEM((HERE, LAT, TOK), F32),
            pltpu.VMEM((2, LAT, TOK), F32),
            pltpu.VMEM((ROW, LAT + 16, TOK), BF),
            pltpu.VMEM((SEQ, LAT + 16, TOK), BF),
            pltpu.VMEM((LAT, TOK), BF),
            pltpu.VMEM((LAT, TOK), BF),
            pltpu.VMEM((LAT, TOK), BF),
            dma((10,)),
            dma((3,)),
            dma((HERE,)), dma((HERE,)), dma((2,)),
            dma((HERE,)), dma((HERE, 3)),
            dma((HERE, 2)), dma((HERE, 2)),
            dma(()), dma((3,)),
            dma((2,)), dma((2,)),
            dma(()), dma(()),
            dma((2,)), dma((2,)),
        ],
        compiler_params=pltpu.CompilerParams(
            collective_id=0, has_side_effects=True, vmem_limit_bytes=60 * 2**20
        ),
    )(
        queries, keys, values, fwd_index, fwd_weight, own_map, back_index, back_weight,
        head_gain.reshape(1, -1), head_shift.reshape(1, -1), head_weight.T, latents,
        eye_mix.reshape(1, -1),
    )


def solution(mesh):
    placed = (
        P("view", "eye", "seq", None),
        P("view", "eye", "seq", None),
        P("view", "eye", "seq", None),
        P("view", "eye", None, None),
        P("view", "eye", None, None),
        P("view", "eye", None, None),
        P("view", "eye", None, None),
        P("view", "eye", None, None),
        P(),
        P(),
        P(),
        P("view", "eye", None, "seq"),
        P(),
    )
    return jax.shard_map(
        local, mesh=mesh, in_specs=placed, out_specs=P("view", "eye", None, "seq"), check_vma=False
    )
```

```python
import math

import jax
import jax.numpy as jnp
from jax import lax
from jax.experimental import pallas as pl
from jax.experimental.pallas import tpu as pltpu
from jax.sharding import PartitionSpec as P

DH = 128
TOK = 128
SEQ = 8
ROW = 8
HERE = 4
FEAT = HERE * DH
LAT = 64
PACK = 40
MESH = pl.DeviceIdType.MESH
BF = jnp.bfloat16
F32 = jnp.float32


def dot(a, b, dims):
    return lax.dot_general(a, b, (dims, ((), ())), preferred_element_type=F32)


def split(x):
    upper = x.astype(BF)
    return upper, (x - upper.astype(F32)).astype(BF)


def wait(ref, sem):
    pltpu.make_async_copy(ref, ref, sem).wait()


def spread(index, weight, rows):
    places = lax.broadcasted_iota(jnp.int32, (rows, TOK), 0).astype(F32)
    total = jnp.zeros((rows, TOK), F32)
    for tap in range(4):
        total = total + jnp.where(places == index[tap : tap + 1], weight[tap : tap + 1], 0.0)
    return total


def kernel(
    q, k, v, fi_in, fw_in, om_in, bi_in, bw_in, gain_in, shift_in, hw_in, lat_in, mix_in, out,
    fi, fw, om, bi, bw, gain, shift, hw, lat, mix,
    kvq, heads, att, ext, pks, pk, vt, jt, mt, acc, stats, wg, gsum, hsum, cols, sp, rp, vsb, vown, voth,
    ins, ks, xs, xr, xq, zs, zr, ys, yr, ps, pr, pys, pyr, rs, rr, fs, fr,
):
    view, eye, seq = lax.axis_index("view"), lax.axis_index("eye"), lax.axis_index("seq")
    row, z = view // ROW, view % ROW
    first = row * ROW
    edge = (z + 2) // 4
    nxt, prv = (view + ROW) % 32, (view + 32 - ROW) % 32
    partner = {"view": first + seq, "eye": eye, "seq": z}
    across = {"view": first + seq, "eye": 1 - eye, "seq": z}

    def along_seq(i):
        return {"view": view, "eye": eye, "seq": i}

    def along_view(i):
        return {"view": i, "eye": eye, "seq": seq}

    def send(src, dst, s, r, target):
        pltpu.make_async_remote_copy(
            src_ref=src, dst_ref=dst, send_sem=s, recv_sem=r, device_id=target, device_id_type=MESH
        ).start()

    def copy(src, dst, s):
        pltpu.make_async_copy(src, dst, s).start()

    small = (
        (fi_in, fi), (fw_in, fw), (om_in, om), (bi_in, bi), (bw_in, bw),
        (gain_in, gain), (shift_in, shift), (hw_in, hw), (lat_in, lat), (mix_in, mix),
    )
    for t, src in enumerate((k, v, q)):
        copy(src.at[0, 0], kvq.at[t], ks.at[t])
    barrier = pltpu.get_barrier_semaphore()

    def greet(target):
        pl.semaphore_signal(barrier, inc=1, device_id=target, device_id_type=MESH)

    for step in range(1, SEQ):
        greet(along_seq((seq + step) % SEQ))
        greet(along_view(first + (z + step) % ROW))
    greet(along_view(nxt))
    greet(along_view(prv))
    greet(across)

    @pl.when(z != seq)
    def _():
        greet(partner)

    for i, (src, dst) in enumerate(small):
        copy(src, dst, ins.at[i])

    pl.semaphore_wait(barrier, 2 * (SEQ - 1) + 3 + jnp.where(z == seq, 0, 1))

    chip, core = seq // 2, seq % 2

    def send_head(h):
        last = h == HERE - 1
        for side in range(2):
            for begin, count in ((0, 2), (2, 1)) if last else ((0, 3),):
                for step in (1, 3, 2, 0):
                    other = (chip + step) % 4 * 2 + side
                    start = pl.multiple_of((other * HERE + h) * DH, DH)
                    block = kvq.at[begin : begin + count, :, pl.ds(start, DH)]
                    place = heads.at[h, begin : begin + count, seq]
                    sem = xr.at[h] if begin == 0 else xq.at[0 if step in (1, 3) else 1]
                    if step > 0:
                        send(block, place, xs.at[h], sem, along_seq(other))
                        continue

                    @pl.when(core != side)
                    def _():
                        send(block, place, xs.at[h], sem, along_seq(other))

                    @pl.when(core == side)
                    def _():
                        copy(block, place, sem)

    for t in range(3):
        wait(kvq.at[t], ks.at[t])
    send_head(0)
    send_head(1)

    for i, (src, dst) in enumerate(small):
        pltpu.make_async_copy(src, dst, ins.at[i]).wait()

    fwd_raw, back_raw = fw[0, 0], bw[0, 0]
    fwd_norm = fwd_raw / jnp.sum(fwd_raw, axis=0, keepdims=True)
    back_norm = back_raw / jnp.sum(back_raw, axis=0, keepdims=True)
    fwd_place, back_place = fi[0, 0].astype(F32), bi[0, 0].astype(F32)
    present = om[0, 0].astype(F32)
    for g in range(SEQ):
        for tile in range(3):
            at = (g * 3 + tile) * TOK
            pks[g, tile * 4 : tile * 4 + 4, :] = fwd_place[:, at : at + TOK]
            pks[g, 12 + tile * 4 : 16 + tile * 4, :] = fwd_norm[:, at : at + TOK]
        at = g * TOK
        pks[g, 24:28, :] = back_place[:, at : at + TOK]
        pks[g, 28:32, :] = back_norm[:, at : at + TOK]
        pks[g, 32:34, :] = present[:, at : at + TOK]
        pks[g, 34:40, :] = jnp.zeros((6, TOK), F32)
    copy(pks.at[z], pk.at[2 + z], pr.at[edge])

    def send_pack(step, _):
        other = (z + step) % ROW
        send(pks.at[other], pk.at[2 + z], ps, pr.at[edge], along_view(first + other))
        return 0

    lax.fori_loop(1, ROW, send_pack, 0)


    def head_sums(c, carry):
        at = pl.multiple_of(c * FEAT, FEAT)
        turned = hw[:, pl.ds(at, FEAT)].astype(F32)
        gained = jnp.sum(turned * gain[:, pl.ds(at, FEAT)], axis=1, keepdims=True)
        gsum[c] = jnp.broadcast_to(gained, (LAT, TOK))
        return carry + jnp.sum(turned * shift[:, pl.ds(at, FEAT)], axis=1, keepdims=True)

    shift_sum = lax.fori_loop(0, SEQ, head_sums, jnp.zeros((LAT, 1), F32))
    for h in range(HERE):
        at = pl.multiple_of((seq * HERE + h) * DH, DH)
        scaled = hw[:, pl.ds(at, DH)].astype(F32) * gain[:, pl.ds(at, DH)]
        wg[h] = jnp.concatenate(split(scaled), axis=0)
        hsum[h] = jnp.broadcast_to(jnp.sum(scaled, axis=1, keepdims=True), (LAT, TOK))
    diagonal = lax.broadcasted_iota(jnp.int32, (LAT, LAT), 0) == lax.broadcasted_iota(
        jnp.int32, (LAT, LAT), 1
    )
    mix_col = jnp.sum(
        jnp.where(diagonal, jnp.broadcast_to(mix[...], (LAT, LAT)), 0.0), axis=1, keepdims=True
    )
    cols[0] = jnp.broadcast_to(shift_sum, (LAT, TOK))
    cols[1] = jnp.broadcast_to(mix_col, (LAT, TOK))

    rate = math.log2(math.e) / math.sqrt(DH)

    def query_blocks(h, groups):
        keyed = heads[h, 0].reshape(SEQ * TOK, DH)
        rows = [jnp.concatenate([heads[h, 2, g] for g in groups[i : i + 2]], axis=0) for i in (0, 2)]
        scores = [dot(keyed, r, ((1,), (1,))) for r in rows]
        highest = [jnp.max(x, axis=0, keepdims=True) for x in scores]
        probs = [jnp.exp2((x - m) * rate) for x, m in zip(scores, highest)]
        total = [jnp.sum(p, axis=0, keepdims=True) for p in probs]
        mixed = [dot(vt[...], p.astype(BF), ((1,), (0,))) for p in probs]
        mixed = [(m / t).astype(BF) for m, t in zip(mixed, total)]
        for i, g in enumerate(groups):
            att[h, g] = mixed[i // 2][:, i % 2 * TOK : (i % 2 + 1) * TOK]

    def send_group(h, g):
        send(att.at[h, g], ext.at[h, 2 + z], zs.at[h], zr.at[h, edge], along_view(first + g))

    def keep_group(h, g):
        copy(att.at[h, g], ext.at[h, 2 + z], zr.at[h, edge])

    def attend(h):
        wait(heads.at[h], xr.at[h])
        vt[...] = heads[h, 1].reshape(SEQ * TOK, DH).T

        def one(step, _):
            groups = [(z + 1 + 4 * step + i) % SEQ for i in range(4)]
            query_blocks(h, groups)
            for g in groups[:3]:
                send_group(h, g)
            pl.when(step == 0)(lambda: send_group(h, groups[3]))
            pl.when(step == 1)(lambda: keep_group(h, groups[3]))
            return 0

        lax.fori_loop(0, 2, one, 0)

    def attend_last(h):
        wait(heads.at[h, 0:2], xr.at[h])
        vt[...] = heads[h, 1].reshape(SEQ * TOK, DH).T
        for i, steps in enumerate(((1, 3), (2, 0))):
            wait(heads.at[h, 2, 0:4], xq.at[i])
            groups = [(chip + step) % 4 * 2 + side for step in steps for side in range(2)]
            query_blocks(h, groups)
            for g in groups:
                pl.when(g != z)(lambda g=g: send_group(h, g))
                pl.when(g == z)(lambda g=g: keep_group(h, g))

    def join(u):
        a0, a1 = pk[u + 1, 32:33, :], pk[u + 1, 33:34, :]
        share = 1.0 / (1.0 + a0 + a1)
        for i, factor in enumerate((a0 * share, share, a1 * share)):
            tile = 2 - i
            part = spread(
                pk[u + i, tile * 4 : tile * 4 + 4, :],
                pk[u + i, 12 + tile * 4 : 16 + tile * 4, :] * factor,
                TOK,
            )
            upper, lower = split(part)
            jt[u, i * TOK : (i + 1) * TOK, :] = upper
            jt[u, (3 + i) * TOK : (4 + i) * TOK, :] = lower


    def compose(w):
        back = spread(pk[w + 2, 24:28, :], pk[w + 2, 28:32, :], 3 * TOK)
        parts = [jnp.zeros((TOK, TOK), F32) for _ in range(5)]
        for b in range(3):
            upper, lower = split(back[b * TOK : (b + 1) * TOK])
            wide = dot(jt[w + b], jnp.concatenate([upper, lower], axis=1), ((1,), (0,)))
            wide = wide[:, :TOK] + wide[:, TOK:]
            wide = wide[: 3 * TOK] + wide[3 * TOK :]
            for i in range(3):
                parts[b + i] = parts[b + i] + wide[i * TOK : (i + 1) * TOK]
        for i in range(5):
            upper, lower = split(parts[i])
            mt[w, i * TOK : (i + 1) * TOK, :TOK] = upper
            mt[w, i * TOK : (i + 1) * TOK, TOK:] = lower

    def in_pairs(count, step):
        def two(i, _):
            step(2 * i)
            step(2 * i + 1)
            return 0

        lax.fori_loop(0, count // 2, two, 0)

    def blend(h, views):
        wide = [
            dot(jnp.concatenate([ext[h, w + i] for i in range(5)], axis=1), mt[w], ((1,), (0,)))
            for w in views
        ]
        x = [a[:, :TOK] + a[:, TOK:] for a in wide]
        mean = [jnp.sum(a, axis=0, keepdims=True) * (1.0 / DH) for a in x]
        centred = [a - m for a, m in zip(x, mean)]
        squares = [jnp.sum(a * a, axis=0, keepdims=True) for a in centred]
        wide = dot(wg[h], jnp.concatenate([a.astype(BF) for a in centred], axis=1), ((1,), (0,)))
        wide = wide[:LAT] + wide[LAT:]
        part = [wide[:, i * TOK : (i + 1) * TOK] for i in range(len(views))]
        if h > 0:
            part = [a + acc[w] for a, w in zip(part, views)]
        for a, m, w in zip(squares, mean, views):
            stats[w, h : h + 1, :] = m
            stats[w, HERE + h : HERE + h + 1, :] = a
        if h < HERE - 1:
            for a, w in zip(part, views):
                acc[w] = a
            return

        for part_here, w in zip(part, views):
            means = stats[w, 0:HERE, :]
            middle = jnp.sum(means, axis=0, keepdims=True) * (1.0 / HERE)
            apart = means - middle
            summed = jnp.sum(stats[w, HERE:, :] + DH * apart * apart, axis=0, keepdims=True)
            for i in range(HERE):
                part_here = part_here + hsum[i] * apart[i : i + 1]
            rows = []
            for line in (middle, summed):
                for _ in range(3):
                    piece = line.astype(BF).astype(F32)
                    rows.append(piece)
                    line = line - piece
            rows.append(jnp.zeros((10, TOK), F32))
            sp[w, 0:LAT, :] = part_here.astype(BF)
            sp[w, LAT:, :] = jnp.concatenate(rows, axis=0).astype(BF)
        for w in views:

            @pl.when(w != seq)
            def _():
                send(sp.at[w], rp.at[seq], rs, rr, along_seq(w))

            @pl.when(w == seq)
            def _():
                copy(sp.at[w], rp.at[seq], rr)

    def forward(h):
        wait(ext.at[h, 8:10], zr.at[h, 2])
        send(ext.at[h, 8:10], ext.at[h, 0:2], ys.at[h, 0], yr.at[h, 0], along_view(nxt))
        wait(ext.at[h, 2:4], zr.at[h, 0])
        send(ext.at[h, 2:4], ext.at[h, 10:12], ys.at[h, 1], yr.at[h, 1], along_view(prv))

    def finish(h):
        wait(ext.at[h, 4:8], zr.at[h, 1])
        blend(h, (2, 3, 4, 5))
        wait(ext.at[h, 0:2], yr.at[h, 0])
        wait(ext.at[h, 10:12], yr.at[h, 1])
        blend(h, (0, 1, 6, 7))

    attend(0)
    send_head(2)

    wait(pk.at[2:4], pr.at[0])
    wait(pk.at[8:10], pr.at[2])
    send(pk.at[8:10], pk.at[0:2], pys.at[0], pyr.at[0], along_view(nxt))
    send(pk.at[2:4], pk.at[10:12], pys.at[1], pyr.at[1], along_view(prv))

    attend(1)
    send_head(3)
    wait(pk.at[4:8], pr.at[1])
    wait(pk.at[0:2], pyr.at[0])
    wait(pk.at[10:12], pyr.at[1])
    in_pairs(ROW + 2, join)
    attend(2)
    in_pairs(ROW, compose)
    forward(0)
    finish(0)
    forward(1)
    attend_last(3)
    forward(2)
    finish(1)
    finish(2)
    forward(3)
    finish(3)
    wait(rp, rr)
    pieces = rp[:, LAT:, :].astype(F32)
    means = pieces[:, 0] + pieces[:, 1] + pieces[:, 2]
    squares = pieces[:, 3] + pieces[:, 4] + pieces[:, 5]
    mean = jnp.sum(means, axis=0, keepdims=True) * (1.0 / SEQ)
    apart = means - mean
    squares = jnp.sum(squares + FEAT * apart * apart, axis=0, keepdims=True)
    deviation = jnp.sqrt(squares * (1.0 / (SEQ * FEAT)) + 1e-06)
    summed = jnp.zeros((LAT, TOK), F32)
    for i in range(SEQ):
        summed = summed + (rp[i, :LAT, :].astype(F32) + gsum[i] * apart[i : i + 1])
    velocity = summed / deviation + cols[0]
    vsb[...] = velocity.astype(BF)
    send(vsb, voth, fs.at[1], fr.at[1], across)

    @pl.when(z != seq)
    def _():
        send(vsb, vown, fs.at[0], fr.at[0], partner)

    @pl.when(z == seq)
    def _():
        copy(vsb, vown, fr.at[0])

    for h in range(HERE):
        wait(heads.at[h, :, 0 : SEQ - 1], xs.at[h])
        wait(att.at[h, 0 : ROW - 1], zs.at[h])
        wait(ext.at[h, 8:10], ys.at[h, 0])
        wait(ext.at[h, 2:4], ys.at[h, 1])
    wait(pks.at[0 : ROW - 1], ps)
    wait(pk.at[8:10], pys.at[0])
    wait(pk.at[2:4], pys.at[1])
    wait(sp.at[0 : SEQ - 1], rs)

    wait(vown, fr.at[0])
    wait(voth, fr.at[1])
    mine = vown[...].astype(F32)
    out[0, 0] = lat[0, 0] - 0.8 * (mine + cols[1] * (voth[...].astype(F32) - mine))

    wait(vsb, fs.at[1])

    @pl.when(z != seq)
    def _():
        wait(vsb, fs.at[0])


def local(
    queries, keys, values, fwd_index, fwd_weight, own_map, back_index, back_weight,
    head_gain, head_shift, head_weight, latents, eye_mix,
):
    hbm = pl.BlockSpec(memory_space=pltpu.HBM)
    vmem = pl.BlockSpec(memory_space=pltpu.VMEM)
    dma = pltpu.SemaphoreType.DMA
    block = (TOK, DH)
    return pl.pallas_call(
        kernel,
        out_shape=jax.ShapeDtypeStruct((1, 1, LAT, TOK), F32),
        in_specs=[hbm] * 13,
        out_specs=vmem,
        scratch_shapes=[
            pltpu.VMEM(fwd_index.shape, jnp.int32),
            pltpu.VMEM(fwd_weight.shape, F32),
            pltpu.VMEM(own_map.shape, jnp.int32),
            pltpu.VMEM(back_index.shape, jnp.int32),
            pltpu.VMEM(back_weight.shape, F32),
            pltpu.VMEM((1, SEQ * FEAT), F32),
            pltpu.VMEM((1, SEQ * FEAT), F32),
            pltpu.VMEM((LAT, SEQ * FEAT), BF),
            pltpu.VMEM((1, 1, LAT, TOK), F32),
            pltpu.VMEM((1, LAT), F32),
            pltpu.VMEM((3, TOK, SEQ * FEAT), BF),
            pltpu.VMEM((HERE, 3, SEQ) + block, BF),
            pltpu.VMEM((HERE, SEQ) + block, BF),
            pltpu.VMEM((HERE, ROW + 4) + block, BF),
            pltpu.VMEM((SEQ, PACK, TOK), F32),
            pltpu.VMEM((ROW + 4, PACK, TOK), F32),
            pltpu.VMEM((DH, SEQ * TOK), BF),
            pltpu.VMEM((ROW + 2, 6 * TOK, TOK), BF),
            pltpu.VMEM((ROW, 5 * TOK, 2 * TOK), BF),
            pltpu.VMEM((ROW, LAT, TOK), F32),
            pltpu.VMEM((ROW, 2 * HERE, TOK), F32),
            pltpu.VMEM((HERE, 2 * LAT, DH), BF),
            pltpu.VMEM((SEQ, LAT, TOK), F32),
            pltpu.VMEM((HERE, LAT, TOK), F32),
            pltpu.VMEM((2, LAT, TOK), F32),
            pltpu.VMEM((ROW, LAT + 16, TOK), BF),
            pltpu.VMEM((SEQ, LAT + 16, TOK), BF),
            pltpu.VMEM((LAT, TOK), BF),
            pltpu.VMEM((LAT, TOK), BF),
            pltpu.VMEM((LAT, TOK), BF),
            dma((10,)),
            dma((3,)),
            dma((HERE,)), dma((HERE,)), dma((2,)),
            dma((HERE,)), dma((HERE, 3)),
            dma((HERE, 2)), dma((HERE, 2)),
            dma(()), dma((3,)),
            dma((2,)), dma((2,)),
            dma(()), dma(()),
            dma((2,)), dma((2,)),
        ],
        compiler_params=pltpu.CompilerParams(
            collective_id=0, has_side_effects=True, vmem_limit_bytes=60 * 2**20
        ),
    )(
        queries, keys, values, fwd_index, fwd_weight, own_map, back_index, back_weight,
        head_gain.reshape(1, -1), head_shift.reshape(1, -1), head_weight.T, latents,
        eye_mix.reshape(1, -1),
    )


def solution(mesh):
    placed = (
        P("view", "eye", "seq", None),
        P("view", "eye", "seq", None),
        P("view", "eye", "seq", None),
        P("view", "eye", None, None),
        P("view", "eye", None, None),
        P("view", "eye", None, None),
        P("view", "eye", None, None),
        P("view", "eye", None, None),
        P(),
        P(),
        P(),
        P("view", "eye", None, "seq"),
        P(),
    )
    return jax.shard_map(
        local, mesh=mesh, in_specs=placed, out_specs=P("view", "eye", None, "seq"), check_vma=False
    )
```
